256 devices in a mesh: view: 2 (over y_lo), tm: 8 (over x, core), head: 16 (over z, y_hi).
Axes of the slice: x: 4, y: 4 (y_hi: 2, y_lo: 2; y = y_hi * 2 + y_lo), z: 8, core: 2. Of those that a mesh axis runs over, the one named last changes fastest.
Arguments:
- tokens: bfloat16 [4, 1024, 5120], P('view', ('tm', 'head')), may hold values from -16 to 16, as said below
- query_weight: bfloat16 [5120, 4096], P(('view', 'tm'), 'head'), as said below
- key_weight: bfloat16 [5120, 4096], P(('view', 'tm'), 'head'), as said below
- value_weight: bfloat16 [5120, 4096], P(('view', 'tm'), 'head'), may hold values from -0.078125 to 0.078125
- out_grad: bfloat16 [4, 1024, 4096], P('view', 'tm', 'head'), may hold values from -6 to 6
- pairs: int32 [5, 2], replicated, may hold values from 0 to 3, as said below
- block_masks: int32 [4, 16], replicated, may hold values from 0 to 1, as said below
Outputs:
- attended: bfloat16 [4, 1024, 4096], P('view', 'tm', 'head')
- token_grad: bfloat16 [4, 1024, 5120], P('view', ('tm', 'head'))
- query_weight_grad: bfloat16 [5120, 4096], P(('view', 'tm'), 'head')
- key_weight_grad: bfloat16 [5120, 4096], P(('view', 'tm'), 'head')
- value_weight_grad: bfloat16 [5120, 4096], P(('view', 'tm'), 'head')
The draws below stay inside these ranges and needn't reach their ends.
Inputs may be any that keep to these rules, and one draw needn't show every extreme that they name: `tokens`: row scales may differ from token to token. `query_weight`: entries of order 5120 ** -0.5. `key_weight`: entries of order 5120 ** -0.5. `pairs`: each row (i, j) has i < j; rows are distinct; every camera appears in two or more rows. `block_masks`: every camera has at least one block equal to 1.
All inputs are finite; a program needn't handle non-finite values.
Results may differ from the reference program's by a relative error of at most 0.04.
Values may be sent and summed in bfloat16 or wider, within the bound.
A program may use at most 128 MiB of HBM per device.

```python
import math
import jax
import jax.numpy as jnp
from jax import lax

D = 5120
HEAD_SIZE = 128
CAM_DEV = 2
TOK_DEV = 128
HEADS = 32
HD = 4096
CAMS = 4
CAM_TOK = 1024
MASK_SPAN = 64
MBLOCKS = 16
N_VIEW = 2
N_TM = 8
N_HEAD = 16


def draw_tokens(key, part):
    key = jax.random.fold_in(key, 11)
    first = jax.random.fold_in(key, 0)
    return jnp.clip(jax.random.normal(first, (CAMS, CAM_TOK, D), jnp.float32), -6.0, 6.0).astype(jnp.bfloat16)


def draw_query_weight(key, part):
    key = jax.random.fold_in(key, 21)
    own = jnp.clip(jax.random.normal(key, (D, HD), jnp.float32), -6.0, 6.0)
    return (own / math.sqrt(D)).astype(jnp.bfloat16)


def draw_key_weight(key, part):
    key = jax.random.fold_in(key, 22)
    own = jnp.clip(jax.random.normal(key, (D, HD), jnp.float32), -6.0, 6.0)
    return (own / math.sqrt(D)).astype(jnp.bfloat16)


def draw_pairs(key, part):
    key = jax.random.fold_in(key, 41)
    order = jax.random.permutation(key, CAMS).astype(jnp.int32)
    nxt = jnp.roll(order, -1)
    first = jnp.concatenate((order, order[0:1]))
    second = jnp.concatenate((nxt, order[2:3]))
    low = jnp.minimum(first, second)
    high = jnp.maximum(first, second)
    return jnp.stack((low, high), axis=1).astype(jnp.int32)


def draw_block_masks(key, part):
    key = jax.random.fold_in(key, 31)
    first, second = jax.random.split(key)
    ones = jax.random.randint(first, (CAMS, MBLOCKS), 0, 2)
    forced = jax.random.randint(second, (CAMS, 1), 0, MBLOCKS)
    slots = jnp.arange(MBLOCKS, dtype=jnp.int32)[None, :]
    return jnp.maximum(ones, (slots == forced).astype(jnp.int32)).astype(jnp.int32)


def shard_levels(key, extent, shards, least, largest):
    level, own = 1.0, jax.random.fold_in(key, 6)
    for axis_at, blocks in shards:
        heights = jnp.exp(jax.random.uniform(jax.random.fold_in(own, axis_at), (blocks,), jnp.float32, least / len(shards), largest / len(shards)))
        level = level * jnp.repeat(heights, extent[axis_at] // blocks).reshape([-1 if axis == axis_at else 1 for axis in range(len(extent))])
    return level


def normal_values(key, extent, spread, reach, shards=(), kind=jnp.bfloat16):
    values = spread * jax.random.normal(key, extent, jnp.float32)
    if shards:
        values = values * shard_levels(key, extent, shards, -0.22, 0.18)
    return jnp.clip(values, -reach, reach).astype(kind)


def setup_inputs(seed: int = 0) -> dict:
    seeds = jax.random.split(jax.random.key(seed), 8)
    return {
        "tokens": draw_tokens(jax.random.fold_in(seeds[7], 71), 0),
        "query_weight": draw_query_weight(jax.random.fold_in(seeds[7], 71), 0),
        "key_weight": draw_key_weight(jax.random.fold_in(seeds[7], 71), 0),
        "value_weight": normal_values(seeds[3], (D, HD), D ** -0.5, 0.078125, ((0, 16), (1, 16))),
        "out_grad": normal_values(seeds[4], (CAMS, CAM_TOK, HD), 1.0, 6.0, ((0, 2), (1, 8), (2, 16))),
        "pairs": draw_pairs(jax.random.fold_in(seeds[7], 71), 0),
        "block_masks": draw_block_masks(jax.random.fold_in(seeds[7], 71), 0),
    }


def rounded(values):
    return lax.optimization_barrier(values.astype(jnp.bfloat16)).astype(jnp.float32)

def allowed_keys(pairs, block_masks):
    ids = jnp.arange(CAMS, dtype=jnp.int32)
    first = pairs[:, 0][:, None, None]
    second = pairs[:, 1][:, None, None]
    row_ids = ids[None, :, None]
    col_ids = ids[None, None, :]
    hits = (first == row_ids) & (second == col_ids) | (first == col_ids) & (second == row_ids)
    linked = lax.optimization_barrier(jnp.max(hits.astype(jnp.int32), axis=0))
    blocks = jnp.arange(CAM_TOK, dtype=jnp.int32) // MASK_SPAN
    open_keys = block_masks[:, blocks]
    return (linked[:, :, None] * open_keys[None, :, :]).reshape(CAMS, CAMS * CAM_TOK)

def grouped(array):
    width = array.shape[-1]
    shaped = array.reshape(N_VIEW, CAM_DEV, N_TM, TOK_DEV, width).transpose(0, 2, 1, 3, 4)
    return shaped.reshape(N_VIEW * N_TM, CAM_DEV * TOK_DEV, width)

def ungrouped(array):
    width = array.shape[-1]
    shaped = array.reshape(N_VIEW, N_TM, CAM_DEV, TOK_DEV, width).transpose(0, 2, 1, 3, 4)
    return shaped.reshape(CAMS * CAM_TOK, width)

def reference(tokens, query_weight, key_weight, value_weight, out_grad, pairs, block_masks):
    scale = 1.0 / math.sqrt(HEAD_SIZE)
    total_rows = CAMS * CAM_TOK
    groups = N_VIEW * N_TM
    group_rows = CAM_DEV * TOK_DEV
    flat = tokens.reshape(total_rows, D)
    query = jnp.dot(flat, query_weight, preferred_element_type=jnp.float32).astype(jnp.bfloat16)
    key = jnp.dot(flat, key_weight, preferred_element_type=jnp.float32).astype(jnp.bfloat16)
    value = jnp.dot(flat, value_weight, preferred_element_type=jnp.float32).astype(jnp.bfloat16)
    allowed = allowed_keys(pairs, block_masks)
    row_cams = jnp.repeat(jnp.arange(CAMS, dtype=jnp.int32), CAM_TOK)
    allow_rows = grouped(allowed[row_cams]) > 0
    query_heads = grouped(query).reshape(groups, group_rows, HEADS, HEAD_SIZE).transpose(2, 0, 1, 3)
    grad_heads = grouped(out_grad.reshape(total_rows, HD)).reshape(groups, group_rows, HEADS, HEAD_SIZE).transpose(2, 0, 1, 3)
    key_heads = key.reshape(total_rows, HEADS, HEAD_SIZE).transpose(1, 0, 2)
    value_heads = value.reshape(total_rows, HEADS, HEAD_SIZE).transpose(1, 0, 2)

    def one_head(inputs):
        q_head, g_head, k_head, v_head = inputs

        def one_group(carry, group_inputs):
            key_acc, value_acc = carry
            q_rows, g_rows, allow = group_inputs
            raw = jnp.dot(q_rows, k_head.T, preferred_element_type=jnp.float32) * scale
            top = lax.optimization_barrier(jnp.max(jnp.where(allow, raw, -1e+30), axis=1, keepdims=True))
            total = lax.optimization_barrier(jnp.sum(jnp.exp(jnp.where(allow, raw - top, -jnp.inf)), axis=1, keepdims=True))
            log_total = top + jnp.log(total)
            weights = jnp.exp(jnp.where(allow, raw - log_total, -jnp.inf))
            probs = weights.astype(jnp.bfloat16)
            attended = jnp.dot(probs, v_head, preferred_element_type=jnp.float32).astype(jnp.bfloat16)
            delta = lax.optimization_barrier(jnp.sum(g_rows.astype(jnp.float32) * attended.astype(jnp.float32), axis=1, keepdims=True))
            dprob = jnp.dot(g_rows, v_head.T, preferred_element_type=jnp.float32)
            dscore = (weights * (dprob - delta) * scale).astype(jnp.bfloat16)
            q_grad = jnp.dot(dscore, k_head, preferred_element_type=jnp.float32).astype(jnp.bfloat16)
            key_part = rounded(jnp.dot(dscore.T, q_rows, preferred_element_type=jnp.float32))
            value_part = rounded(jnp.dot(probs.T, g_rows, preferred_element_type=jnp.float32))
            return ((key_acc + key_part, value_acc + value_part), (attended, q_grad))
        zeros = jnp.zeros((total_rows, HEAD_SIZE), jnp.float32)
        (key_acc, value_acc), (attended, q_grad) = lax.scan(one_group, (zeros, zeros), (q_head, g_head, allow_rows))
        return (attended, q_grad, key_acc.astype(jnp.bfloat16), value_acc.astype(jnp.bfloat16))
    attended_h, qgrad_h, kgrad_h, vgrad_h = lax.map(one_head, (query_heads, grad_heads, key_heads, value_heads))
    attended = ungrouped(attended_h.transpose(1, 2, 0, 3).reshape(groups, group_rows, HD))
    query_grad = ungrouped(qgrad_h.transpose(1, 2, 0, 3).reshape(groups, group_rows, HD))
    key_grad = kgrad_h.transpose(1, 0, 2).reshape(total_rows, HD)
    value_grad = vgrad_h.transpose(1, 0, 2).reshape(total_rows, HD)
    head_width = HD // N_HEAD

    def head_group(carry, index):
        start = (index * head_width).astype(jnp.int32)

        def part(grad, weight):
            left = lax.dynamic_slice_in_dim(grad, start, head_width, 1)
            right = lax.dynamic_slice_in_dim(weight, start, head_width, 1)
            return lax.dot_general(left, right, (((1,), (1,)), ((), ())), preferred_element_type=jnp.float32)
        term = part(query_grad, query_weight) + part(key_grad, key_weight) + part(value_grad, value_weight)
        return (carry + rounded(term), None)
    token_acc, _ = lax.scan(head_group, jnp.zeros((total_rows, D), jnp.float32), jnp.arange(N_HEAD, dtype=jnp.int32))
    token_grad = token_acc.astype(jnp.bfloat16).reshape(CAMS, CAM_TOK, D)
    stacked = grouped(jnp.concatenate((query_grad, key_grad, value_grad), axis=1))
    token_groups = grouped(flat)

    def weight_group(carry, inputs):
        rows_in, grads_in = inputs
        term = lax.dot_general(rows_in, grads_in, (((0,), (0,)), ((), ())), preferred_element_type=jnp.float32)
        return (carry + rounded(term), None)
    weight_acc, _ = lax.scan(weight_group, jnp.zeros((D, 3 * HD), jnp.float32), (token_groups, stacked))
    weight_grads = weight_acc.astype(jnp.bfloat16)
    attended = attended.reshape(CAMS, CAM_TOK, HD)
    return (attended, token_grad, weight_grads[:, :HD], weight_grads[:, HD:2 * HD], weight_grads[:, 2 * HD:])
```

```python
import math

import jax
import jax.numpy as jnp
from jax import lax
from jax.experimental import pallas as pl
from jax.experimental.pallas import tpu as pltpu
from jax.sharding import PartitionSpec as P

MESH = pl.DeviceIdType.MESH
F32 = jnp.float32
BF16 = jnp.bfloat16
VMEM_LIMIT = 58 * 1024 * 1024

HALF = 2560
ROWS = 512
SCALE = 1.0 / math.sqrt(128)
CLOSED = -1e30


class Place:
    def __init__(self):
        self.v = lax.axis_index("view")
        self.t = lax.axis_index("tm")
        self.h = lax.axis_index("head")
        v, t, h = self.v, self.t, self.h
        self.x, self.core = t // 2, lax.rem(t, 2)
        self.z, self.y = h // 2, lax.rem(h, 2)
        self.sib_t = t + 1 - 2 * self.core
        other_h = h + 1 - 2 * self.y
        self.V = {"view": 1 - v}
        self.Y = {"head": other_h}
        self.D = {"view": 1 - v, "head": other_h}
        self.ZP = {"head": lax.rem(h + 2, 16)}
        self.ZM = {"head": lax.rem(h + 14, 16)}
        self.XP = {"tm": lax.rem(t + 2, 8)}
        self.XM = {"tm": lax.rem(t + 6, 8)}
        self.S = {"tm": self.sib_t}

    def greet(self):
        bar = pltpu.get_barrier_semaphore()
        peers = (self.V, self.Y, self.D, self.ZP, self.ZM, self.XP, self.XM, self.S)
        for peer in peers:
            pl.semaphore_signal(bar, inc=1, device_id=peer, device_id_type=MESH)
        pl.semaphore_wait(bar, len(peers))


def rcopy(src, dst, ss, rs, dev):
    return pltpu.make_async_remote_copy(
        src_ref=src, dst_ref=dst, send_sem=ss, recv_sem=rs, device_id=dev, device_id_type=MESH
    )


def lanes(start, size):
    return pl.ds(pl.multiple_of(start, 128), size)


class RingGather:
    def __init__(self, pc, at, ss, rs):
        self.pc, self.at, self.ss, self.rs = pc, at, ss, rs
        self.sent = []

    def cp(self, i, t, half, dev):
        ref = self.at(t, half)
        return rcopy(ref, ref, self.ss.at[i], self.rs.at[i], dev)

    def send(self, i, off, half, dev):
        c = self.cp(i, lax.rem(self.pc.t + off, 8), half, dev)
        c.start()
        self.sent.append(c)

    def recv(self, i, off, half):
        self.cp(i, lax.rem(self.pc.t + off, 8), half, self.pc.S).wait_recv()

    def recv_sib(self, i, off, half):
        self.cp(i, lax.rem(self.pc.sib_t + off, 8), half, self.pc.S).wait_recv()

    def start(self):
        pc = self.pc
        self.send(0, 0, 0, pc.XP)
        self.send(3, 0, 1, pc.XM)
        self.send(1, 0, 1, pc.XP)
        self.send(2, 0, 0, pc.XM)
        self.send(4, 0, 0, pc.S)
        self.send(5, 0, 1, pc.S)

    def first(self):
        pc = self.pc
        self.recv(0, 6, 0)
        self.send(6, 6, 0, pc.XP)
        self.recv(3, 2, 1)
        self.send(7, 2, 1, pc.XM)
        self.send(8, 6, 0, pc.S)
        self.send(11, 2, 1, pc.S)
        self.recv(1, 6, 1)
        self.send(9, 6, 1, pc.S)
        self.recv(2, 2, 0)
        self.send(10, 2, 0, pc.S)

    def second(self):
        pc = self.pc
        self.recv(6, 4, 0)
        self.send(12, 4, 0, pc.S)
        self.recv(7, 4, 1)
        self.send(13, 4, 1, pc.S)

    def finish(self):
        for i, off, half in (
            (4, 0, 0), (5, 0, 1), (8, 6, 0), (9, 6, 1), (10, 2, 0), (11, 2, 1), (12, 4, 0), (13, 4, 1),
        ):
            self.recv_sib(i, off, half)

    def end(self):
        for c in self.sent:
            c.wait_send()


def project_kernel(
    tok, wq, wk, wv, dout,
    X, W, Q, DO, KV,
    stage, kept, part_s, part_r,
    sw_s, sw_r, do_s, do_r, z_s, z_r, w_s, w_r, k_s, k_r, p_s, p_r,
):
    pc = Place()
    v, t, z, y = pc.v, pc.t, pc.z, pc.y
    pc.greet()
    swaps = []
    for k, (dev, vv) in enumerate(((pc.V, 1 - v), (pc.Y, v), (pc.D, 1 - v))):
        c = rcopy(tok.at[:, lanes(vv * HALF, HALF)], stage.at[v, y], sw_s.at[k], sw_r.at[k], dev)
        c.start()
        swaps.append(c)
    W[0, t] = wq[...]
    W[1, t] = wk[...]
    W[2, t] = wv[...]

    def w_at(tt, half):
        return W.at[:, tt, pl.ds(half * 160, 160)]

    wring = RingGather(pc, w_at, w_s, w_r)
    wring.start()
    stage[v, y] = tok[:, lanes(v * HALF, HALF)]
    do_copy = rcopy(
        dout.at[:, :, lanes((1 - v) * 128, 128)], DO.at[pl.ds(2 * v, 2)], do_s, do_r, pc.V
    )
    do_copy.start()
    DO[pl.ds(2 * v, 2)] = dout[:, :, lanes(v * 128, 128)]

    y2 = 1 - y
    for k, (a, b) in enumerate(((1 - v, y), (v, y2), (1 - v, y2))):
        rcopy(stage.at[a, b], stage.at[a, b], sw_s.at[k], sw_r.at[k], pc.V).wait_recv()
    for vv in range(2):
        low = stage[vv, 0].astype(F32)
        high = stage[vv, 1].astype(F32)
        for c in range(2):
            both = jnp.concatenate((low[8 * c : 8 * c + 8], high[8 * c : 8 * c + 8]), axis=0)
            X[2 * vv + c, z] = both.astype(BF16)

    z_sent = []

    def steps(d, cam):
        return 4 if (d == 0) == (cam < 2) else 3

    def z_ref(d, s, cam):
        off = (8 - s) if d == 0 else s
        return X.at[cam, lax.rem(z + off, 8)]

    def z_send(d, s, cam):
        ref = z_ref(d, s - 1, cam)
        c = rcopy(ref, ref, z_s.at[d, s - 1, cam], z_r.at[d, s - 1, cam], pc.ZP if d == 0 else pc.ZM)
        c.start()
        z_sent.append(c)

    def z_open(pair):
        for cam in (2 * pair, 2 * pair + 1):
            for d in range(2):
                z_send(d, 1, cam)

    def z_step(pair, s):
        for cam in (2 * pair, 2 * pair + 1):
            for d in range(2):
                if s <= steps(d, cam):
                    ref = z_ref(d, s, cam)
                    rcopy(ref, ref, z_s.at[d, s - 1, cam], z_r.at[d, s - 1, cam], pc.ZP).wait_recv()
                    if s < steps(d, cam):
                        z_send(d, s + 1, cam)

    p_sent = []

    def project(pair):
        rows = X[2 * pair : 2 * pair + 2].reshape(256, HALF)

        def one(m, carry):
            acc = jnp.dot(rows, W[m].reshape(HALF, 256), preferred_element_type=F32)
            left, right = acc[:, :128], acc[:, 128:]
            part_s[pair, m] = jnp.where(v == 0, right, left).astype(BF16)
            kept[pair, m] = jnp.where(v == 0, left, right)
            return carry

        lax.fori_loop(0, 3, one, 0)
        c = rcopy(part_s.at[pair], part_r.at[pair], p_s.at[pair], p_r.at[pair], pc.V)
        c.start()
        p_sent.append(c)

    def merge(pair):
        rcopy(part_s.at[pair], part_r.at[pair], p_s.at[pair], p_r.at[pair], pc.V).wait_recv()
        cams = slice(2 * pair, 2 * pair + 2)
        for m in range(3):
            whole = (kept[pair, m] + part_r[pair, m].astype(F32)).astype(BF16).reshape(2, 128, 128)
            if m == 0:
                Q[cams] = whole
            else:
                KV[m - 1, cams, t] = whole

    def kv_at(pair):
        return lambda tt, half: KV.at[half, pl.ds(2 * pair, 2), tt]

    kvrings = [RingGather(pc, kv_at(p), k_s.at[p], k_r.at[p]) for p in range(2)]

    z_open(0)
    z_step(0, 1)
    z_step(0, 2)
    z_step(0, 3)
    z_open(1)
    wring.first()
    z_step(0, 4)
    z_step(1, 1)
    wring.second()
    z_step(1, 2)
    wring.finish()
    project(0)
    z_step(1, 3)
    merge(0)
    kvrings[0].start()
    z_step(1, 4)
    project(1)
    kvrings[0].first()
    merge(1)
    kvrings[1].start()
    kvrings[0].second()
    kvrings[1].first()
    kvrings[1].second()
    kvrings[0].finish()
    kvrings[1].finish()
    do_copy.wait_recv()
    for ring in (wring, *kvrings):
        ring.end()
    for c in (*swaps, do_copy, *z_sent, *p_sent):
        c.wait_send()


def attend_kernel(pairs, masks, q_in, g_in, kv, att, dq, dkv, kc, vc, s_buf, dkc, dvc, bias, blk):
    for j in range(4):
        for i in range(4):
            hit = jnp.int32(0)
            for r in range(5):
                a, b = pairs[r, 0], pairs[r, 1]
                one = jnp.logical_or(
                    jnp.logical_and(a == i, b == j), jnp.logical_and(a == j, b == i)
                )
                hit = hit + one.astype(jnp.int32)
            level = jnp.where(hit > 0, 0.0, CLOSED).astype(F32)
            bias[pl.ds(j, 1), pl.ds(128 * i, 128)] = jnp.full((1, 128), level, F32)
    bias[pl.ds(4, 1), :] = jnp.full((1, ROWS), CLOSED, F32)

    def block64(n):
        return pl.ds(pl.multiple_of(n * 64, 64), 64)

    def squeeze(b, n):
        j, s = b // 16, lax.rem(b, 16)
        is_open = masks[j, s] > 0

        @pl.when(is_open)
        def _():
            kc[block64(n)] = kv[0, j, s // 2, block64(lax.rem(s, 2))]
            vc[block64(n)] = kv[1, j, s // 2, block64(lax.rem(s, 2))]
            blk[n] = j

        return n + is_open.astype(jnp.int32)

    count = lax.fori_loop(0, 64, squeeze, jnp.int32(0))
    chunks = (count + 3) // 4
    for e in range(3):

        @pl.when(count + e < 4 * chunks)
        def _():
            kc[block64(count + e)] = jnp.zeros((64, 128), BF16)
            vc[block64(count + e)] = jnp.zeros((64, 128), BF16)
            blk[count + e] = 4

    q = q_in[...].reshape(ROWS, 128)
    g = g_in[...].reshape(ROWS, 128)

    def chunk(c):
        return pl.ds(pl.multiple_of(c * 256, 256), 256)

    def nt(a, b):
        return lax.dot_general(a, b, (((1,), (1,)), ((), ())), preferred_element_type=F32)

    def tn(a, b):
        return lax.dot_general(a, b, (((0,), (0,)), ((), ())), preferred_element_type=F32)

    def score(c, top):
        s = nt(kc[chunk(c)], q) * SCALE
        parts = [s[64 * e : 64 * e + 64] + bias[pl.ds(blk[4 * c + e], 1), :] for e in range(4)]
        s = jnp.concatenate(parts, axis=0)
        s_buf[chunk(c)] = s
        return jnp.maximum(top, jnp.max(s, axis=0, keepdims=True))

    top = lax.fori_loop(0, chunks, score, jnp.full((1, ROWS), CLOSED, F32))

    def expo(c, total):
        e = jnp.exp(s_buf[chunk(c)] - top)
        s_buf[chunk(c)] = e
        return total + jnp.sum(e, axis=0, keepdims=True)

    total = lax.fori_loop(0, chunks, expo, jnp.zeros((1, ROWS), F32))
    inv = 1.0 / total

    def mix(c, acc):
        p = (s_buf[chunk(c)] * inv).astype(BF16)
        return acc + tn(vc[chunk(c)], p)

    mixed = lax.fori_loop(0, chunks, mix, jnp.zeros((128, ROWS), F32))
    out = jnp.transpose(mixed).astype(BF16)
    att[...] = out.reshape(4, 128, 128)
    prod = out.astype(F32) * g.astype(F32)
    delta = jnp.sum(jnp.transpose(prod), axis=0, keepdims=True)

    def back(c, acc):
        w = s_buf[chunk(c)] * inv
        dp = nt(vc[chunk(c)], g)
        ds = (w * (dp - delta) * SCALE).astype(BF16)
        dkc[chunk(c)] = jnp.dot(ds, q, preferred_element_type=F32).astype(BF16)
        dvc[chunk(c)] = jnp.dot(w.astype(BF16), g, preferred_element_type=F32).astype(BF16)
        return acc + tn(kc[chunk(c)], ds)

    dq_t = lax.fori_loop(0, chunks, back, jnp.zeros((128, ROWS), F32))
    dq[...] = jnp.transpose(dq_t).astype(BF16).reshape(4, 128, 128)

    def spread(b, n):
        j, s = b // 16, lax.rem(b, 16)
        is_open = masks[j, s] > 0

        @pl.when(is_open)
        def _():
            dkv[0, j, s // 2, block64(lax.rem(s, 2))] = dkc[block64(n)]
            dkv[1, j, s // 2, block64(lax.rem(s, 2))] = dvc[block64(n)]

        @pl.when(jnp.logical_not(is_open))
        def _():
            dkv[0, j, s // 2, block64(lax.rem(s, 2))] = jnp.zeros((64, 128), BF16)
            dkv[1, j, s // 2, block64(lax.rem(s, 2))] = jnp.zeros((64, 128), BF16)

        return n + is_open.astype(jnp.int32)

    lax.fori_loop(0, 64, spread, jnp.int32(0))


class RingScatter:
    def __init__(self, pc, own, sib_src, sib_r, bufs, bufr, ss, rs):
        self.pc, self.own, self.sib_src, self.sib_r = pc, own, sib_src, sib_r
        self.bufs, self.bufr, self.ss, self.rs = bufs, bufr, ss, rs
        self.sent = []

    def sib_cp(self, k):
        return rcopy(self.sib_src(k), self.sib_r.at[k], self.ss.at[6 + k], self.rs.at[6 + k], self.pc.S)

    def sib_send(self, k):
        c = self.sib_cp(k)
        c.start()
        self.sent.append(c)

    def sib_wait(self, k):
        self.sib_cp(k).wait_recv()

    def cp(self, i, dev):
        return rcopy(self.bufs.at[i], self.bufr.at[i], self.ss.at[i], self.rs.at[i], dev)

    def term(self, k, half):
        return self.own(k, half) + self.sib_r[k, half].astype(F32)

    def push(self, i, value, dev):
        self.bufs[i] = value.astype(BF16)
        c = self.cp(i, dev)
        c.start()
        self.sent.append(c)

    def wait(self, i):
        self.cp(i, self.pc.S).wait_recv()
        return self.bufr[i].astype(F32)

    def far(self):
        self.sib_wait(0)
        self.push(0, self.term(0, 0), self.pc.XP)
        self.push(1, self.term(0, 1), self.pc.XM)

    def near(self):
        self.sib_wait(1)
        self.push(3, self.term(1, 1), self.pc.XP)
        self.sib_wait(2)
        self.push(4, self.term(2, 0), self.pc.XM)

    def near2(self):
        self.push(2, self.term(1, 0) + self.wait(0), self.pc.XP)
        self.push(5, self.term(2, 1) + self.wait(1), self.pc.XM)

    def last(self, half):
        if half == 0:
            self.sib_wait(3)
        return self.term(3, half) + self.wait(2 + half) + self.wait(4 + half)

    def end(self):
        for c in self.sent:
            c.wait_send()


def grads_kernel(
    X, W, att, dq, dkv,
    att_out, tgrad, gq, gk, gv,
    G, TG, zbs, zbr, fin, ys, yr, sib1, b1s, b1r, wt, sib2s, sib2r, b2s, b2r,
    a_s, a_r, e_s, e_r, z_s, z_r, y_s, y_r, d_s, d_r, w_s, w_r,
):
    pc = Place()
    v, z, y, x, core = pc.v, pc.z, pc.y, pc.x, pc.core
    pc.greet()
    sent = []

    def go(c):
        c.start()
        sent.append(c)

    def shifted(k):
        return lax.rem(x + (2, 1, 3, 0)[k], 4)

    dring = RingScatter(
        pc,
        lambda k, half: dkv[half, :, 2 * shifted(k) + core].astype(F32),
        lambda k: dkv.at[:, :, 2 * shifted(k) + 1 - core],
        sib1, b1s, b1r, d_s, d_r,
    )
    for k in range(4):
        dring.sib_send(k)
    own_cols = lanes(v * 128, 128)
    go(rcopy(att.at[pl.ds(2 - 2 * v, 2)], att_out.at[:, :, own_cols], a_s, a_r, pc.V))

    def g_cols(m, head):
        return lanes(m * 256 + head * 128, 128)

    def g_copy(m, head):
        ref = G.at[:, g_cols(m, head)]
        return rcopy(ref, ref, e_s.at[m], e_r.at[m], pc.V)

    dring.far()
    G[:, g_cols(0, v)] = dq[...].reshape(ROWS, 128)
    go(g_copy(0, v))
    att_out[:, :, own_cols] = att[pl.ds(2 * v, 2)]
    dring.near()
    dring.near2()
    for half in range(2):
        G[:, g_cols(1 + half, v)] = dring.last(half).astype(BF16).reshape(ROWS, 128)
        go(g_copy(1 + half, v))
    for m in range(3):
        g_copy(m, 1 - v).wait_recv()

    def token_term(pair):
        rows = G[256 * pair : 256 * pair + 256, :]

        def some(i, carry):
            acc = jnp.zeros((256, 640), F32)
            for m in range(3):
                weight = W[m, pl.ds(2 * i, 2)].reshape(640, 256)
                acc = acc + lax.dot_general(
                    rows[:, 256 * m : 256 * m + 256], weight, (((1,), (1,)), ((), ())),
                    preferred_element_type=F32,
                )
            TG[2 * pair : 2 * pair + 2, :, :, lanes(i * 640, 640)] = acc.reshape(2, 8, 16, 640)
            return carry

        lax.fori_loop(0, 4, some, 0)

    def steps(d, cam):
        return 4 if (d == 0) == (cam < 2) else 3

    def z_cp(d, s, cam):
        return rcopy(
            zbs.at[d, s - 1, cam], zbr.at[d, s - 1, cam], z_s.at[d, s - 1, cam], z_r.at[d, s - 1, cam],
            pc.ZP if d == 0 else pc.ZM,
        )

    def z_step(pair, s):
        for cam in (2 * pair, 2 * pair + 1):
            for d in range(2):
                n = steps(d, cam)
                if s <= n:
                    far = n - s + 1
                    value = TG[cam, lax.rem(z + (far if d == 0 else 8 - far), 8)]
                    if s > 1:
                        z_cp(d, s - 1, cam).wait_recv()
                        value = value + zbr[d, s - 2, cam].astype(F32)
                    zbs[d, s - 1, cam] = value.astype(BF16)
                    go(z_cp(d, s, cam))

    def z_last(pair):
        for cam in (2 * pair, 2 * pair + 1):
            value = TG[cam, z]
            for d in range(2):
                n = steps(d, cam)
                z_cp(d, n, cam).wait_recv()
                value = value + zbr[d, n - 1, cam].astype(F32)
            fin[cam] = value

    def w_own(k, half):
        return wt[k, :, pl.ds(half * 160, 160)]

    wring = RingScatter(pc, w_own, lambda k: sib2s.at[k], sib2r, b2s, b2r, w_s, w_r)

    def weight_term(k):
        cols = X[:, :, :, lanes(shifted(k) * 640, 640)].reshape(ROWS, 640)
        for m in range(3):
            acc = lax.dot_general(
                cols, G[:, 256 * m : 256 * m + 256], (((0,), (0,)), ((), ())),
                preferred_element_type=F32,
            )
            low, high = acc[:320], acc[320:]
            wt[k, m] = jnp.where(core == 0, low, high)
            other = jnp.where(core == 0, high, low).astype(BF16)
            sib2s[k, 0, m] = other[:160]
            sib2s[k, 1, m] = other[160:]
        wring.sib_send(k)

    token_term(0)
    z_step(0, 1)
    token_term(1)
    z_step(1, 1)
    weight_term(0)
    weight_term(1)
    wring.far()
    z_step(0, 2)
    z_step(1, 2)
    weight_term(2)
    wring.near()
    z_step(0, 3)
    z_step(1, 3)
    weight_term(3)
    wring.near2()
    z_step(0, 4)
    z_step(1, 4)
    z_last(0)
    z_last(1)

    def piece(vv, yy):
        rows = pl.ds(pl.multiple_of(8 * yy, 8), 8)
        return jnp.concatenate((fin[2 * vv, rows], fin[2 * vv + 1, rows]), axis=0)

    def y_cp(k):
        return rcopy(ys.at[k], yr.at[k], y_s.at[k], y_r.at[k], (pc.V, pc.Y, pc.D)[k])

    for k, (vv, yy) in enumerate(((1 - v, y), (v, 1 - y), (1 - v, 1 - y))):
        ys[k] = piece(vv, yy).astype(BF16)
        go(y_cp(k))
    for half in range(2):
        value = wring.last(half)
        rows = slice(160 * half, 160 * half + 160)
        for m, out in enumerate((gq, gk, gv)):
            out[rows] = value[m].astype(BF16)
    for k in range(3):
        y_cp(k).wait_recv()
    tgrad[:, lanes(v * HALF, HALF)] = (piece(v, y) + yr[1].astype(F32)).astype(BF16)
    tgrad[:, lanes((1 - v) * HALF, HALF)] = (yr[0].astype(F32) + yr[2].astype(F32)).astype(BF16)
    rcopy(att.at[pl.ds(2 - 2 * v, 2)], att_out.at[:, :, lanes((1 - v) * 128, 128)], a_s, a_r, pc.V).wait_recv()
    for ring in (dring, wring):
        ring.end()
    for c in sent:
        c.wait_send()


def on_device(tokens, query_weight, key_weight, value_weight, out_grad, pairs, block_masks):
    vm = pl.BlockSpec(memory_space=pltpu.VMEM)
    sm = pl.BlockSpec(memory_space=pltpu.SMEM)
    dma = pltpu.SemaphoreType.DMA

    def shape(*dims):
        return jax.ShapeDtypeStruct(dims, BF16)

    X, W, Q, DO, KV = pl.pallas_call(
        project_kernel,
        out_shape=(
            shape(4, 8, 16, HALF), shape(3, 8, 320, 256), shape(4, 128, 128), shape(4, 128, 128),
            shape(2, 4, 8, 128, 128),
        ),
        in_specs=[vm] * 5,
        out_specs=[vm] * 5,
        scratch_shapes=[
            pltpu.VMEM((2, 2, 16, HALF), BF16),
            pltpu.VMEM((2, 3, 256, 128), F32),
            pltpu.VMEM((2, 3, 256, 128), BF16),
            pltpu.VMEM((2, 3, 256, 128), BF16),
            dma((3,)), dma((3,)), dma, dma,
            dma((2, 4, 4)), dma((2, 4, 4)),
            dma((14,)), dma((14,)), dma((2, 14)), dma((2, 14)), dma((2,)), dma((2,)),
        ],
        compiler_params=pltpu.CompilerParams(
            collective_id=0, has_side_effects=True, vmem_limit_bytes=VMEM_LIMIT
        ),
        name="project",
    )(tokens.reshape(16, 2 * HALF), query_weight, key_weight, value_weight, out_grad)

    att, dq, dkv = pl.pallas_call(
        attend_kernel,
        out_shape=(shape(4, 128, 128), shape(4, 128, 128), shape(2, 4, 8, 128, 128)),
        in_specs=[sm, sm, vm, vm, vm],
        out_specs=[vm] * 3,
        scratch_shapes=[
            pltpu.VMEM((4096, 128), BF16),
            pltpu.VMEM((4096, 128), BF16),
            pltpu.VMEM((4096, ROWS), F32),
            pltpu.VMEM((4096, 128), BF16),
            pltpu.VMEM((4096, 128), BF16),
            pltpu.VMEM((8, ROWS), F32),
            pltpu.SMEM((64,), jnp.int32),
        ],
        compiler_params=pltpu.CompilerParams(vmem_limit_bytes=VMEM_LIMIT),
        name="attend",
    )(pairs, block_masks, Q, DO, KV)

    att_out, tgrad, gq, gk, gv = pl.pallas_call(
        grads_kernel,
        out_shape=(
            shape(2, 128, 256), shape(16, 2 * HALF), shape(320, 256), shape(320, 256), shape(320, 256),
        ),
        in_specs=[vm] * 5,
        out_specs=[vm] * 5,
        scratch_shapes=[
            pltpu.VMEM((ROWS, 768), BF16),
            pltpu.VMEM((4, 8, 16, HALF), F32),
            pltpu.VMEM((2, 4, 4, 16, HALF), BF16),
            pltpu.VMEM((2, 4, 4, 16, HALF), BF16),
            pltpu.VMEM((4, 16, HALF), F32),
            pltpu.VMEM((3, 16, HALF), BF16),
            pltpu.VMEM((3, 16, HALF), BF16),
            pltpu.VMEM((4, 2, 4, 128, 128), BF16),
            pltpu.VMEM((6, 4, 128, 128), BF16),
            pltpu.VMEM((6, 4, 128, 128), BF16),
            pltpu.VMEM((4, 3, 320, 256), F32),
            pltpu.VMEM((4, 2, 3, 160, 256), BF16),
            pltpu.VMEM((4, 2, 3, 160, 256), BF16),
            pltpu.VMEM((6, 3, 160, 256), BF16),
            pltpu.VMEM((6, 3, 160, 256), BF16),
            dma, dma, dma((3,)), dma((3,)),
            dma((2, 4, 4)), dma((2, 4, 4)), dma((3,)), dma((3,)),
            dma((10,)), dma((10,)), dma((10,)), dma((10,)),
        ],
        compiler_params=pltpu.CompilerParams(
            collective_id=1, has_side_effects=True, vmem_limit_bytes=VMEM_LIMIT
        ),
        name="grads",
    )(X, W, att, dq, dkv)
    return (att_out, tgrad.reshape(2, 8, 2 * HALF), gq, gk, gv)


def solution(mesh):
    return jax.shard_map(
        on_device,
        mesh=mesh,
        in_specs=(
            P("view", ("tm", "head"), None),
            P(("view", "tm"), "head"),
            P(("view", "tm"), "head"),
            P(("view", "tm"), "head"),
            P("view", "tm", "head"),
            P(),
            P(),
        ),
        out_specs=(
            P("view", "tm", "head"),
            P("view", ("tm", "head"), None),
            P(("view", "tm"), "head"),
            P(("view", "tm"), "head"),
            P(("view", "tm"), "head"),
        ),
        check_vma=False,
    )
```

```python
import math

import jax
import jax.numpy as jnp
from jax import lax
from jax.experimental import pallas as pl
from jax.experimental.pallas import tpu as pltpu
from jax.sharding import PartitionSpec as P

MESH = pl.DeviceIdType.MESH
F32 = jnp.float32
BF16 = jnp.bfloat16
VMEM_LIMIT = 58 * 1024 * 1024

HALF = 2560
ROWS = 512
SCALE = 1.0 / math.sqrt(128)
CLOSED = -1e30
Z_STEPS = ((4, 3), (3, 4), (4, 3))
LOG2E = math.log2(math.e)


class Place:
    def __init__(self):
        self.v = lax.axis_index("view")
        self.t = lax.axis_index("tm")
        self.h = lax.axis_index("head")
        v, t, h = self.v, self.t, self.h
        self.x, self.core = t // 2, lax.rem(t, 2)
        self.z, self.y = h // 2, lax.rem(h, 2)
        self.sib_t = t + 1 - 2 * self.core
        other_h = h + 1 - 2 * self.y
        self.V = {"view": 1 - v}
        self.Y = {"head": other_h}
        self.D = {"view": 1 - v, "head": other_h}
        self.ZP = {"head": lax.rem(h + 2, 16)}
        self.ZM = {"head": lax.rem(h + 14, 16)}
        self.XP = {"tm": lax.rem(t + 2, 8)}
        self.XM = {"tm": lax.rem(t + 6, 8)}
        self.S = {"tm": self.sib_t}

    def greet(self):
        bar = pltpu.get_barrier_semaphore()
        peers = (self.V, self.Y, self.D, self.ZP, self.ZM, self.XP, self.XM, self.S)
        for peer in peers:
            pl.semaphore_signal(bar, inc=1, device_id=peer, device_id_type=MESH)
        pl.semaphore_wait(bar, len(peers))


def rcopy(src, dst, ss, rs, dev):
    return pltpu.make_async_remote_copy(
        src_ref=src, dst_ref=dst, send_sem=ss, recv_sem=rs, device_id=dev, device_id_type=MESH
    )


def lanes(start, size):
    return pl.ds(pl.multiple_of(start, 128), size)


class RingGather:
    def __init__(self, pc, at, ss, rs):
        self.pc, self.at, self.ss, self.rs = pc, at, ss, rs
        self.sent = []

    def cp(self, i, t, half, dev):
        ref = self.at(t, half)
        return rcopy(ref, ref, self.ss.at[i], self.rs.at[i], dev)

    def send(self, i, off, half, dev):
        c = self.cp(i, lax.rem(self.pc.t + off, 8), half, dev)
        c.start()
        self.sent.append(c)

    def recv(self, i, off, half):
        self.cp(i, lax.rem(self.pc.t + off, 8), half, self.pc.S).wait_recv()

    def recv_sib(self, i, off, half):
        self.cp(i, lax.rem(self.pc.sib_t + off, 8), half, self.pc.S).wait_recv()

    def start(self):
        pc = self.pc
        self.send(0, 0, 0, pc.XP)
        self.send(3, 0, 1, pc.XM)
        self.send(1, 0, 1, pc.XP)
        self.send(2, 0, 0, pc.XM)
        self.send(4, 0, 0, pc.S)
        self.send(5, 0, 1, pc.S)

    def first(self):
        pc = self.pc
        self.recv(0, 6, 0)
        self.send(6, 6, 0, pc.XP)
        self.recv(3, 2, 1)
        self.send(7, 2, 1, pc.XM)
        self.send(8, 6, 0, pc.S)
        self.send(11, 2, 1, pc.S)
        self.recv(1, 6, 1)
        self.send(9, 6, 1, pc.S)
        self.recv(2, 2, 0)
        self.send(10, 2, 0, pc.S)

    def second(self):
        pc = self.pc
        self.recv(6, 4, 0)
        self.send(12, 4, 0, pc.S)
        self.recv(7, 4, 1)
        self.send(13, 4, 1, pc.S)

    def finish(self):
        for i, off, half in (
            (4, 0, 0), (5, 0, 1), (8, 6, 0), (9, 6, 1), (10, 2, 0), (11, 2, 1), (12, 4, 0), (13, 4, 1),
        ):
            self.recv_sib(i, off, half)

    def end(self):
        for c in self.sent:
            c.wait_send()


class RingScatter:
    def __init__(self, pc, own, sib_src, sib_r, bufs, bufr, ss, rs):
        self.pc, self.own, self.sib_src, self.sib_r = pc, own, sib_src, sib_r
        self.bufs, self.bufr, self.ss, self.rs = bufs, bufr, ss, rs
        self.sent = []

    def sib_cp(self, k):
        return rcopy(self.sib_src(k), self.sib_r.at[k], self.ss.at[6 + k], self.rs.at[6 + k], self.pc.S)

    def sib_send(self, k):
        c = self.sib_cp(k)
        c.start()
        self.sent.append(c)

    def sib_wait(self, k):
        self.sib_cp(k).wait_recv()

    def cp(self, i, dev):
        return rcopy(self.bufs.at[i], self.bufr.at[i], self.ss.at[i], self.rs.at[i], dev)

    def term(self, k, half):
        return self.own(k, half) + self.sib_r[k, half].astype(F32)

    def push(self, i, value, dev):
        self.bufs[i] = value.astype(BF16)
        c = self.cp(i, dev)
        c.start()
        self.sent.append(c)

    def wait(self, i):
        self.cp(i, self.pc.S).wait_recv()
        return self.bufr[i].astype(F32)

    def far(self):
        self.sib_wait(0)
        self.push(0, self.term(0, 0), self.pc.XP)
        self.push(1, self.term(0, 1), self.pc.XM)

    def near(self):
        self.sib_wait(1)
        self.push(3, self.term(1, 1), self.pc.XP)
        self.sib_wait(2)
        self.push(4, self.term(2, 0), self.pc.XM)

    def near2(self):
        self.push(2, self.term(1, 0) + self.wait(0), self.pc.XP)
        self.push(5, self.term(2, 1) + self.wait(1), self.pc.XM)

    def last(self, half):
        if half == 0:
            self.sib_wait(3)
        return self.term(3, half) + self.wait(2 + half) + self.wait(4 + half)

    def end(self):
        for c in self.sent:
            c.wait_send()


def fused_kernel(
    tok, wq, wk, wv, dout, pairs, masks,
    att_out, tgrad, gq, gk, gv,
    X, W, Q, DO, KV, stage, kept, part_s, part_r, relay,
    link, bias, s_buf, ds_buf, tops, stat, acc, att, dkv,
    G, TG, zbs, zbr, fin, ys, yr, sib1, b1s, b1r, wt, sib2s, sib2r, b2s, b2r,
    sw_s, sw_r, do_s, do_r, z_s, z_r, w_s, w_r, k_s, k_r, p_s, p_r, r_s, r_r,
    a_s, a_r, e_s, e_r, t_s, t_r, y_s, y_r, d_s, d_r, f_s, f_r,
):
    pc = Place()
    v, t, z, y, x, core = pc.v, pc.t, pc.z, pc.y, pc.x, pc.core
    pc.greet()
    swaps = []
    for k, (dev, vv) in enumerate(((pc.V, 1 - v), (pc.Y, v), (pc.D, 1 - v))):
        c = rcopy(tok.at[:, lanes(vv * HALF, HALF)], stage.at[v, y], sw_s.at[k], sw_r.at[k], dev)
        c.start()
        swaps.append(c)
    W[0, t] = wq[...]
    W[1, t] = wk[...]
    W[2, t] = wv[...]

    def w_at(tt, half):
        return W.at[:, tt, pl.ds(half * 160, 160)]

    wring = RingGather(pc, w_at, w_s, w_r)
    wring.start()
    stage[v, y] = tok[:, lanes(v * HALF, HALF)]
    do_copy = rcopy(
        dout.at[:, :, lanes((1 - v) * 128, 128)], DO.at[pl.ds(2 * v, 2)], do_s, do_r, pc.V
    )
    do_copy.start()
    DO[pl.ds(2 * v, 2)] = dout[:, :, lanes(v * 128, 128)]

    def make_bias():
        for j in range(4):
            for i in range(4):
                hit = jnp.int32(0)
                for r in range(5):
                    a, b = pairs[0, r], pairs[1, r]
                    one = jnp.logical_or(
                        jnp.logical_and(a == i, b == j), jnp.logical_and(a == j, b == i)
                    )
                    hit = hit + one.astype(jnp.int32)
                level = jnp.where(hit > 0, 0.0, CLOSED).astype(F32)
                link[pl.ds(j, 1), pl.ds(128 * i, 128)] = jnp.full((1, 128), level, F32)
        for j in range(4):
            for s in range(16):
                level = jnp.where(masks[j, s] > 0, 0.0, CLOSED).astype(F32)
                bias[j, pl.ds(s, 1), :] = link[pl.ds(j, 1), :] + level

    make_bias()
    y2 = 1 - y
    for k, (a, b) in enumerate(((1 - v, y), (v, y2), (1 - v, y2))):
        rcopy(stage.at[a, b], stage.at[a, b], sw_s.at[k], sw_r.at[k], pc.V).wait_recv()
    for vv in range(2):
        low = stage[vv, 0].astype(F32)
        high = stage[vv, 1].astype(F32)
        for c in range(2):
            both = jnp.concatenate((low[8 * c : 8 * c + 8], high[8 * c : 8 * c + 8]), axis=0)
            X[2 * vv + c, z] = both.astype(BF16)

    sent = []
    cam_of = (y, 2, 3)

    def z_block(d, s):
        return lax.rem(z + ((8 - s) if d == 0 else s), 8)

    def z_cp(d, s, u):
        ref = X.at[cam_of[u], z_block(d, s - 1)]
        return rcopy(
            ref, ref, z_s.at[d, s - 1, u], z_r.at[d, s - 1, u], pc.ZP if d == 0 else pc.ZM
        )

    def z_send(d, s, u):
        c = z_cp(d, s, u)
        c.start()
        sent.append(c)

    def z_open(u):
        for d in range(2):
            z_send(d, 1, u)

    def z_step(u, s):
        for d in range(2):
            if s <= Z_STEPS[u][d]:
                ref = X.at[cam_of[u], z_block(d, s)]
                rcopy(ref, ref, z_s.at[d, s - 1, u], z_r.at[d, s - 1, u], pc.ZP).wait_recv()
                if s < Z_STEPS[u][d]:
                    z_send(d, s + 1, u)
                if u == 0:
                    c = rcopy(ref, relay.at[d, s - 1], r_s.at[0, d, s - 1], r_r.at[0, d, s - 1], pc.V)
                    c.start()
                    sent.append(c)

    def relay_on(s):
        for d in range(2):
            if s <= Z_STEPS[0][d]:
                ref = relay.at[d, s - 1]
                rcopy(ref, ref, r_s.at[0, d, s - 1], r_r.at[0, d, s - 1], pc.V).wait_recv()
                there = X.at[y, z_block(d, s)]
                c = rcopy(ref, there, r_s.at[1, d, s - 1], r_r.at[1, d, s - 1], pc.D)
                c.start()
                sent.append(c)

    def relay_end():
        for s in range(1, 5):
            for d in range(2):
                if s <= Z_STEPS[0][d]:
                    ref = X.at[1 - y, z_block(d, s)]
                    rcopy(ref, ref, r_s.at[1, d, s - 1], r_r.at[1, d, s - 1], pc.D).wait_recv()

    def go(c):
        c.start()
        sent.append(c)


    def project(pair):
        def one(m, carry):
            rows = X[2 * pair : 2 * pair + 2].reshape(256, HALF)
            acc = jnp.dot(rows, W[m].reshape(HALF, 256), preferred_element_type=F32)
            left, right = acc[:, :128], acc[:, 128:]
            part_s[pair, m] = jnp.where(v == 0, right, left).astype(BF16)
            kept[pair, m] = jnp.where(v == 0, left, right)
            return carry

        lax.fori_loop(1, 3, one, 0)
        go(p_cp(pair, 1))
        lax.fori_loop(0, 1, one, 0)
        go(p_cp(pair, 0))

    def p_cp(pair, i):
        part = pl.ds(0, 1) if i == 0 else pl.ds(1, 2)
        return rcopy(
            part_s.at[pair, part], part_r.at[pair, part], p_s.at[pair, i], p_r.at[pair, i], pc.V
        )

    def whole(pair, m):
        return (kept[pair, m] + part_r[pair, m].astype(F32)).astype(BF16).reshape(2, 128, 128)

    def merge(pair):
        p_cp(pair, 1).wait_recv()
        for m in (1, 2):
            KV[m - 1, 2 * pair : 2 * pair + 2, t] = whole(pair, m)

    def kv_at(pair):
        return lambda tt, half: KV.at[half, pl.ds(2 * pair, 2), tt]

    kvrings = [RingGather(pc, kv_at(p), k_s.at[p], k_r.at[p]) for p in range(2)]

    def nt(a, b):
        return lax.dot_general(a, b, (((1,), (1,)), ((), ())), preferred_element_type=F32)

    def tn(a, b):
        return lax.dot_general(a, b, (((0,), (0,)), ((), ())), preferred_element_type=F32)

    def keys(m, c):
        return KV[m, c // 2, pl.ds(4 * lax.rem(c, 2), 4)].reshape(512, 128)

    def chunk(c):
        return pl.ds(pl.multiple_of(c * 512, 512), 512)

    def forward(low, high, kp):
        qs = slice(256 * low, 256 * high)
        width = 256 * (high - low)

        def step(c, carry):
            top, total = carry
            s = nt(keys(0, c), Q[2 * low : 2 * high].reshape(width, 128)) * (SCALE * LOG2E)
            block = 8 * lax.rem(c, 2)
            parts = [
                s[64 * e : 64 * e + 64] + bias[c // 2, pl.ds(block + e, 1), qs] for e in range(8)
            ]
            s = jnp.concatenate(parts, axis=0)
            new_top = jnp.maximum(top, jnp.max(s, axis=0, keepdims=True))
            fade = jnp.exp2(top - new_top)
            e = jnp.exp2(s - new_top)
            s_buf[chunk(c), qs] = e
            tops[pl.ds(c, 1), qs] = new_top
            acc[:, qs] = acc[:, qs] * fade + tn(keys(1, c), e.astype(BF16))
            return new_top, total * fade + jnp.sum(e, axis=0, keepdims=True)

        if kp == 0:
            start = (jnp.full((1, width), CLOSED, F32), jnp.zeros((1, width), F32))
            acc[:, qs] = jnp.zeros((128, width), F32)
        else:
            start = (stat[0:1, qs], stat[1:2, qs])
        top, total = lax.fori_loop(4 * kp, 4 * kp + 4, step, start)
        stat[0:1, qs] = top
        stat[1:2, qs] = total

    def settle():
        inv = 1.0 / stat[1:2, :]
        out = jnp.transpose(acc[...] * inv).astype(BF16)
        att[...] = out.reshape(4, 128, 128)
        prod = out.astype(F32) * DO[...].reshape(ROWS, 128).astype(F32)
        acc[...] = jnp.zeros((128, ROWS), F32)
        return inv, jnp.sum(jnp.transpose(prod), axis=0, keepdims=True)

    def back(cam):
        def step(c, carry):
            w = s_buf[chunk(c), :] * (jnp.exp2(tops[pl.ds(c, 1), :] - stat[0:1, :]) * inv)
            g = DO[...].reshape(ROWS, 128)
            dv = jnp.dot(w.astype(BF16), g, preferred_element_type=F32)
            ds = (w * (nt(keys(1, c), g) - delta)).astype(BF16)
            ds_buf[chunk(c), :] = ds
            dk = jnp.dot(ds, Q[...].reshape(ROWS, 128), preferred_element_type=F32) * SCALE
            at = pl.ds(4 * lax.rem(c, 2), 4)
            dkv[0, cam, at] = dk.astype(BF16).reshape(4, 128, 128)
            dkv[1, cam, at] = dv.astype(BF16).reshape(4, 128, 128)
            return carry

        lax.fori_loop(2 * cam, 2 * cam + 2, step, 0)
        for k in range(4):
            drings[cam].sib_send(k)

    def query_back(cam):
        def step(c, carry):
            acc[...] += tn(keys(0, c), ds_buf[chunk(c), :])
            return carry

        lax.fori_loop(2 * cam, 2 * cam + 2, step, 0)

    def merge_query(pair):
        p_cp(pair, 0).wait_recv()
        Q[2 * pair : 2 * pair + 2] = whole(pair, 0)

    z_open(0)
    z_open(1)
    z_step(0, 1)
    z_open(2)
    z_step(0, 2)
    z_step(1, 1)
    relay_on(1)
    wring.first()
    z_step(0, 3)
    z_step(2, 1)
    relay_on(2)
    z_step(0, 4)
    z_step(1, 2)
    relay_on(3)
    z_step(2, 2)
    relay_on(4)
    wring.second()
    z_step(1, 3)
    wring.finish()
    z_step(2, 3)
    relay_end()
    project(0)
    z_step(1, 4)
    z_step(2, 4)
    merge(0)
    kvrings[0].start()
    project(1)
    kvrings[0].first()
    kvrings[0].second()
    merge_query(0)
    do_copy.wait_recv()
    kvrings[0].finish()
    forward(0, 1, 0)
    merge(1)
    kvrings[1].start()
    merge_query(1)
    forward(1, 2, 0)
    kvrings[1].first()
    kvrings[1].second()
    kvrings[1].finish()
    forward(0, 2, 1)
    inv, delta = settle()
    def shifted(k):
        return lax.rem(x + (2, 1, 3, 0)[k], 4)

    def make_dring(p):
        return RingScatter(
            pc,
            lambda k, half: dkv[half, p, 2 * shifted(k) + core].astype(F32),
            lambda k: dkv.at[:, p, 2 * shifted(k) + 1 - core],
            sib1.at[p], b1s.at[p], b1r.at[p], d_s.at[p], d_r.at[p],
        )

    drings = [make_dring(p) for p in range(4)]
    own_cols = lanes(v * 128, 128)

    def g_at(p, m, head):
        return G.at[pl.ds(128 * p, 128), lanes(m * 256 + head * 128, 128)]

    def g_copy(p, m, head):
        ref = g_at(p, m, head)
        return rcopy(ref, ref, e_s.at[p, m], e_r.at[p, m], pc.V)

    def give(p, m, value):
        g_at(p, m, v)[...] = value
        go(g_copy(p, m, v))

    def take(p):
        for cam in (2 * p, 2 * p + 1):
            for m in range(3):
                g_copy(cam, m, 1 - v).wait_recv()

    def hand_on(p):
        for half in range(2):
            give(p, 1 + half, drings[p].last(half).astype(BF16))

    back(0)
    go(rcopy(att.at[pl.ds(2 - 2 * v, 2)], att_out.at[:, :, own_cols], a_s, a_r, pc.V))
    back(1)
    drings[0].far()
    drings[0].near()
    back(2)
    drings[1].far()
    drings[1].near()
    drings[0].near2()
    back(3)
    drings[2].far()
    drings[2].near()
    drings[1].near2()
    hand_on(0)
    query_back(0)
    query_back(1)
    drings[3].far()
    drings[3].near()
    drings[2].near2()
    hand_on(1)
    query_back(2)
    query_back(3)
    drings[3].near2()
    hand_on(2)
    dq = jnp.transpose(acc[...] * SCALE).astype(BF16)
    for p in range(4):
        give(p, 0, dq[128 * p : 128 * p + 128])
    hand_on(3)
    att_out[:, :, own_cols] = att[pl.ds(2 * v, 2)]

    def token_term(pair):
        rows = G[256 * pair : 256 * pair + 256, :]

        def some(i, carry):
            acc = jnp.zeros((256, 640), F32)
            for m in range(3):
                weight = W[m, pl.ds(2 * i, 2)].reshape(640, 256)
                acc = acc + lax.dot_general(
                    rows[:, 256 * m : 256 * m + 256], weight, (((1,), (1,)), ((), ())),
                    preferred_element_type=F32,
                )
            TG[2 * pair : 2 * pair + 2, :, :, lanes(i * 640, 640)] = acc.reshape(2, 8, 16, 640)
            return carry

        lax.fori_loop(0, 4, some, 0)

    def t_steps(d, cam):
        return 4 if (d == 0) == (cam < 2) else 3

    def t_z_cp(d, s, cam):
        return rcopy(
            zbs.at[d, s - 1, cam], zbr.at[d, s - 1, cam], t_s.at[d, s - 1, cam], t_r.at[d, s - 1, cam],
            pc.ZP if d == 0 else pc.ZM,
        )

    def t_z_step(pair, s):
        for cam in (2 * pair, 2 * pair + 1):
            for d in range(2):
                n = t_steps(d, cam)
                if s <= n:
                    far = n - s + 1
                    value = TG[cam, lax.rem(z + (far if d == 0 else 8 - far), 8)]
                    if s > 1:
                        t_z_cp(d, s - 1, cam).wait_recv()
                        value = value + zbr[d, s - 2, cam].astype(F32)
                    zbs[d, s - 1, cam] = value.astype(BF16)
                    go(t_z_cp(d, s, cam))

    def t_z_last(pair):
        for cam in (2 * pair, 2 * pair + 1):
            value = TG[cam, z]
            for d in range(2):
                n = t_steps(d, cam)
                t_z_cp(d, n, cam).wait_recv()
                value = value + zbr[d, n - 1, cam].astype(F32)
            fin[cam] = value

    def g_own(k, half):
        return wt[k, :, pl.ds(half * 160, 160)]

    gring = RingScatter(pc, g_own, lambda k: sib2s.at[k], sib2r, b2s, b2r, f_s, f_r)

    def weight_term(k):
        cols = X[:, :, :, lanes(shifted(k) * 640, 640)].reshape(ROWS, 640)
        for m in range(3):
            acc = lax.dot_general(
                cols, G[:, 256 * m : 256 * m + 256], (((0,), (0,)), ((), ())),
                preferred_element_type=F32,
            )
            low, high = acc[:320], acc[320:]
            wt[k, m] = jnp.where(core == 0, low, high)
            other = jnp.where(core == 0, high, low).astype(BF16)
            sib2s[k, 0, m] = other[:160]
            sib2s[k, 1, m] = other[160:]
        gring.sib_send(k)

    take(0)
    token_term(0)
    t_z_step(0, 1)
    take(1)
    token_term(1)
    t_z_step(1, 1)
    weight_term(0)
    weight_term(1)
    t_z_step(0, 2)
    gring.far()
    weight_term(2)
    t_z_step(1, 2)
    gring.near()
    weight_term(3)
    t_z_step(0, 3)
    t_z_step(1, 3)
    gring.near2()
    t_z_step(0, 4)
    t_z_step(1, 4)
    for half in range(2):
        value = gring.last(half)
        rows = slice(160 * half, 160 * half + 160)
        for m, out in enumerate((gq, gk, gv)):
            out[rows] = value[m].astype(BF16)
    t_z_last(0)
    t_z_last(1)

    def piece(vv, yy):
        rows = pl.ds(pl.multiple_of(8 * yy, 8), 8)
        return jnp.concatenate((fin[2 * vv, rows], fin[2 * vv + 1, rows]), axis=0)

    def y_cp(k):
        return rcopy(ys.at[k], yr.at[k], y_s.at[k], y_r.at[k], (pc.V, pc.Y, pc.D)[k])

    for k, (vv, yy) in enumerate(((1 - v, y), (v, 1 - y), (1 - v, 1 - y))):
        ys[k] = piece(vv, yy).astype(BF16)
        go(y_cp(k))
    for k in range(3):
        y_cp(k).wait_recv()
    tgrad[:, lanes(v * HALF, HALF)] = (piece(v, y) + yr[1].astype(F32)).astype(BF16)
    tgrad[:, lanes((1 - v) * HALF, HALF)] = (yr[0].astype(F32) + yr[2].astype(F32)).astype(BF16)
    rcopy(att.at[pl.ds(2 - 2 * v, 2)], att_out.at[:, :, lanes((1 - v) * 128, 128)], a_s, a_r, pc.V).wait_recv()
    for ring in (wring, *kvrings, *drings, gring):
        ring.end()
    for c in (*swaps, do_copy, *sent):
        c.wait_send()


def hand_over_kernel(*refs):
    ins, outs, held, sems = refs[:5], refs[5:10], refs[10:15], refs[15]
    loads = [pltpu.make_async_copy(ins[i], held[i], sems.at[0, i]) for i in range(5)]
    stores = [pltpu.make_async_copy(held[i], outs[i], sems.at[1, i]) for i in range(5)]
    for c in loads:
        c.start()
    for load, store in zip(loads, stores):
        load.wait()
        store.start()
    for c in stores:
        c.wait()


def on_device(tokens, query_weight, key_weight, value_weight, out_grad, pairs, block_masks):
    vm = pl.BlockSpec(memory_space=pltpu.VMEM)
    sm = pl.BlockSpec(memory_space=pltpu.SMEM)
    hbm = pl.BlockSpec(memory_space=pl.ANY)
    dma = pltpu.SemaphoreType.DMA

    def shape(*dims):
        return jax.ShapeDtypeStruct(dims, BF16)

    def half(*dims):
        return pltpu.VMEM(dims, BF16)

    def full(*dims):
        return pltpu.VMEM(dims, F32)

    outs = pl.pallas_call(
        fused_kernel,
        out_shape=(
            shape(2, 128, 256), shape(16, 2 * HALF), shape(320, 256), shape(320, 256), shape(320, 256),
        ),
        in_specs=[vm] * 5 + [sm] * 2,
        out_specs=[vm] * 5,
        scratch_shapes=[
            half(4, 8, 16, HALF), half(3, 8, 320, 256), half(4, 128, 128), half(4, 128, 128),
            half(2, 4, 8, 128, 128), half(2, 2, 16, HALF), full(2, 3, 256, 128),
            half(2, 3, 256, 128), half(2, 3, 256, 128), half(2, 4, 16, HALF),
            full(8, ROWS), full(4, 16, ROWS), full(4096, ROWS), half(4096, ROWS),
            full(16, ROWS), full(8, ROWS),
            full(128, ROWS), half(4, 128, 128), half(2, 4, 8, 128, 128),
            half(ROWS, 768), full(4, 8, 16, HALF), half(2, 4, 4, 16, HALF), half(2, 4, 4, 16, HALF),
            full(4, 16, HALF), half(3, 16, HALF), half(3, 16, HALF),
            half(4, 4, 2, 128, 128), half(4, 6, 128, 128), half(4, 6, 128, 128),
            full(4, 3, 320, 256), half(4, 2, 3, 160, 256), half(4, 2, 3, 160, 256),
            half(6, 3, 160, 256), half(6, 3, 160, 256),
            dma((3,)), dma((3,)), dma, dma, dma((2, 4, 3)), dma((2, 4, 3)),
            dma((14,)), dma((14,)), dma((2, 14)), dma((2, 14)), dma((2, 2)), dma((2, 2)),
            dma((2, 2, 4)), dma((2, 2, 4)),
            dma, dma, dma((4, 3)), dma((4, 3)), dma((2, 4, 4)), dma((2, 4, 4)), dma((3,)), dma((3,)),
            dma((4, 10)), dma((4, 10)), dma((10,)), dma((10,)),
        ],
        compiler_params=pltpu.CompilerParams(
            collective_id=0, has_side_effects=True, vmem_limit_bytes=VMEM_LIMIT
        ),
        name="fused",
    )(
        tokens.reshape(16, 2 * HALF), query_weight, key_weight, value_weight, out_grad, pairs.T,
        block_masks,
    )

    att_out, tgrad, gq, gk, gv = pl.pallas_call(
        hand_over_kernel,
        out_shape=tuple(jax.ShapeDtypeStruct(a.shape, a.dtype) for a in outs),
        in_specs=[hbm] * 5,
        out_specs=[hbm] * 5,
        scratch_shapes=[*(pltpu.VMEM(a.shape, BF16) for a in outs), dma((2, 5))],
        compiler_params=pltpu.CompilerParams(vmem_limit_bytes=VMEM_LIMIT),
        name="hand_over",
    )(*outs)
    return (att_out, tgrad.reshape(2, 8, 2 * HALF), gq, gk, gv)


def solution(mesh):
    return jax.shard_map(
        on_device,
        mesh=mesh,
        in_specs=(
            P("view", ("tm", "head"), None),
            P(("view", "tm"), "head"),
            P(("view", "tm"), "head"),
            P(("view", "tm"), "head"),
            P("view", "tm", "head"),
            P(),
            P(),
        ),
        out_specs=(
            P("view", "tm", "head"),
            P("view", ("tm", "head"), None),
            P(("view", "tm"), "head"),
            P(("view", "tm"), "head"),
            P(("view", "tm"), "head"),
        ),
        check_vma=False,
    )
```

```python
import math

import jax
import jax.numpy as jnp
from jax import lax
from jax.experimental import pallas as pl
from jax.experimental.pallas import tpu as pltpu
from jax.sharding import PartitionSpec as P

MESH = pl.DeviceIdType.MESH
F32 = jnp.float32
BF16 = jnp.bfloat16
VMEM_LIMIT = 58 * 1024 * 1024

HALF = 2560
ROWS = 512
SCALE = 1.0 / math.sqrt(128)
CLOSED = -1e30
LOG2E = math.log2(math.e)


class Place:
    def __init__(self):
        self.v = lax.axis_index("view")
        self.t = lax.axis_index("tm")
        self.h = lax.axis_index("head")
        v, t, h = self.v, self.t, self.h
        self.x, self.core = t // 2, lax.rem(t, 2)
        self.z, self.y = h // 2, lax.rem(h, 2)
        self.sib_t = t + 1 - 2 * self.core
        other_h = h + 1 - 2 * self.y
        self.V = {"view": 1 - v}
        self.Y = {"head": other_h}
        self.D = {"view": 1 - v, "head": other_h}
        self.ZP = {"head": lax.rem(h + 2, 16)}
        self.ZM = {"head": lax.rem(h + 14, 16)}
        self.XP = {"tm": lax.rem(t + 2, 8)}
        self.XM = {"tm": lax.rem(t + 6, 8)}
        self.S = {"tm": self.sib_t}

    def greet(self):
        bar = pltpu.get_barrier_semaphore()
        peers = (self.V, self.Y, self.D, self.ZP, self.ZM, self.XP, self.XM, self.S)
        for peer in peers:
            pl.semaphore_signal(bar, inc=1, device_id=peer, device_id_type=MESH)
        pl.semaphore_wait(bar, len(peers))


def rcopy(src, dst, ss, rs, dev):
    return pltpu.make_async_remote_copy(
        src_ref=src, dst_ref=dst, send_sem=ss, recv_sem=rs, device_id=dev, device_id_type=MESH
    )


def lanes(start, size):
    return pl.ds(pl.multiple_of(start, 128), size)


class RingGather:
    def __init__(self, pc, at, ss, rs):
        self.pc, self.at, self.ss, self.rs = pc, at, ss, rs
        self.sent = []

    def cp(self, i, t, half, dev):
        ref = self.at(t, half)
        return rcopy(ref, ref, self.ss.at[i], self.rs.at[i], dev)

    def send(self, i, off, half, dev):
        c = self.cp(i, lax.rem(self.pc.t + off, 8), half, dev)
        c.start()
        self.sent.append(c)

    def recv(self, i, off, half):
        self.cp(i, lax.rem(self.pc.t + off, 8), half, self.pc.S).wait_recv()

    def recv_sib(self, i, off, half):
        self.cp(i, lax.rem(self.pc.sib_t + off, 8), half, self.pc.S).wait_recv()

    def start(self):
        pc = self.pc
        self.send(0, 0, 0, pc.XP)
        self.send(3, 0, 1, pc.XM)
        self.send(1, 0, 1, pc.XP)
        self.send(2, 0, 0, pc.XM)
        self.send(4, 0, 0, pc.S)
        self.send(5, 0, 1, pc.S)

    def first(self):
        pc = self.pc
        self.recv(0, 6, 0)
        self.send(6, 6, 0, pc.XP)
        self.recv(3, 2, 1)
        self.send(7, 2, 1, pc.XM)
        self.send(8, 6, 0, pc.S)
        self.send(11, 2, 1, pc.S)
        self.recv(1, 6, 1)
        self.send(9, 6, 1, pc.S)
        self.recv(2, 2, 0)
        self.send(10, 2, 0, pc.S)

    def second(self):
        pc = self.pc
        self.recv(6, 4, 0)
        self.send(12, 4, 0, pc.S)
        self.recv(7, 4, 1)
        self.send(13, 4, 1, pc.S)

    def finish(self):
        for i, off, half in (
            (4, 0, 0), (5, 0, 1), (8, 6, 0), (9, 6, 1), (10, 2, 0), (11, 2, 1), (12, 4, 0), (13, 4, 1),
        ):
            self.recv_sib(i, off, half)

    def end(self):
        for c in self.sent:
            c.wait_send()


class RingScatter:
    def __init__(self, pc, own, sib_src, sib_r, bufs, bufr, ss, rs):
        self.pc, self.own, self.sib_src, self.sib_r = pc, own, sib_src, sib_r
        self.bufs, self.bufr, self.ss, self.rs = bufs, bufr, ss, rs
        self.sent = []

    def sib_cp(self, k):
        return rcopy(self.sib_src(k), self.sib_r.at[k], self.ss.at[6 + k], self.rs.at[6 + k], self.pc.S)

    def sib_send(self, k):
        c = self.sib_cp(k)
        c.start()
        self.sent.append(c)

    def sib_wait(self, k):
        self.sib_cp(k).wait_recv()

    def cp(self, i, dev):
        return rcopy(self.bufs.at[i], self.bufr.at[i], self.ss.at[i], self.rs.at[i], dev)

    def term(self, k, half):
        return self.own(k, half) + self.sib_r[k, half].astype(F32)

    def push(self, i, value, dev):
        self.bufs[i] = value.astype(BF16)
        c = self.cp(i, dev)
        c.start()
        self.sent.append(c)

    def wait(self, i):
        self.cp(i, self.pc.S).wait_recv()
        return self.bufr[i].astype(F32)

    def far(self):
        self.sib_wait(0)
        self.push(0, self.term(0, 0), self.pc.XP)
        self.push(1, self.term(0, 1), self.pc.XM)

    def near(self):
        self.sib_wait(1)
        self.push(3, self.term(1, 1), self.pc.XP)
        self.sib_wait(2)
        self.push(4, self.term(2, 0), self.pc.XM)

    def near2(self):
        self.push(2, self.term(1, 0) + self.wait(0), self.pc.XP)
        self.push(5, self.term(2, 1) + self.wait(1), self.pc.XM)

    def last(self, half):
        if half == 0:
            self.sib_wait(3)
        return self.term(3, half) + self.wait(2 + half) + self.wait(4 + half)

    def end(self):
        for c in self.sent:
            c.wait_send()


def fused_kernel(
    tok, wq, wk, wv, dout, pairs, masks,
    att_out, tgrad, gq, gk, gv,
    X, W, Q, DO, KV, stage, kept, part_s, part_r,
    link, bias, s_buf, ds_buf, tops, stat, acc, att, dkv,
    G, TG, zbs, zbr, fin, ys, yr, sib1, b1s, b1r, wt, sib2s, sib2r, b2s, b2r,
    l_s, sw_s, sw_r, do_s, do_r, z_s, z_r, w_s, w_r, k_s, k_r, p_s, p_r,
    a_s, a_r, e_s, e_r, t_s, t_r, y_s, y_r, d_s, d_r, f_s, f_r,
):
    pc = Place()
    v, t, z, y, x, core = pc.v, pc.t, pc.z, pc.y, pc.x, pc.core
    loads = [
        pltpu.make_async_copy(tok.at[:, lanes(v * HALF, HALF)], stage.at[v, y], l_s.at[0]),
        pltpu.make_async_copy(wq, W.at[0, t], l_s.at[1]),
        pltpu.make_async_copy(wk, W.at[1, t], l_s.at[2]),
        pltpu.make_async_copy(wv, W.at[2, t], l_s.at[3]),
        pltpu.make_async_copy(
            dout.at[:, :, lanes(v * 128, 128)], DO.at[pl.ds(2 * v, 2)], l_s.at[4]
        ),
    ]
    for c in loads:
        c.start()
    pc.greet()
    swaps = []
    sent = []
    y2 = 1 - y
    for k, dev, vv in ((0, pc.V, 1 - v), (2, pc.D, 1 - v), (1, pc.Y, v)):
        c = rcopy(tok.at[:, lanes(vv * HALF, HALF)], stage.at[v, y], sw_s.at[k], sw_r.at[k], dev)
        c.start()
        swaps.append(c)

    def w_at(tt, half):
        return W.at[:, tt, pl.ds(half * 160, 160)]

    for c in loads:
        c.wait()
    wring = RingGather(pc, w_at, w_s, w_r)
    wring.start()
    do_copy = rcopy(
        dout.at[:, :, lanes((1 - v) * 128, 128)], DO.at[pl.ds(2 * v, 2)], do_s, do_r, pc.V
    )
    do_copy.start()

    def make_bias():
        for j in range(4):
            for i in range(4):
                hit = jnp.int32(0)
                for r in range(5):
                    a, b = pairs[0, r], pairs[1, r]
                    one = jnp.logical_or(
                        jnp.logical_and(a == i, b == j), jnp.logical_and(a == j, b == i)
                    )
                    hit = hit + one.astype(jnp.int32)
                level = jnp.where(hit > 0, 0.0, CLOSED).astype(F32)
                link[pl.ds(j, 1), pl.ds(128 * i, 128)] = jnp.full((1, 128), level, F32)
        for j in range(4):
            for s in range(16):
                level = jnp.where(masks[j, s] > 0, 0.0, CLOSED).astype(F32)
                bias[j, pl.ds(s, 1), :] = link[pl.ds(j, 1), :] + level

    make_bias()

    def swapped(k, a, b):
        rcopy(stage.at[a, b], stage.at[a, b], sw_s.at[k], sw_r.at[k], pc.V).wait_recv()

    def assemble(vv):
        low = stage[vv, 0].astype(F32)
        high = stage[vv, 1].astype(F32)
        for c in range(2):
            both = jnp.concatenate((low[8 * c : 8 * c + 8], high[8 * c : 8 * c + 8]), axis=0)
            X[2 * vv + c, z] = both.astype(BF16)

    def steps(d, cam):
        return 4 if (d == 0) == (cam < 2) else 3

    def z_ref(d, s, cam):
        return X.at[cam, lax.rem(z + ((8 - s) if d == 0 else s), 8)]

    def z_send(d, s, cam):
        ref = z_ref(d, s - 1, cam)
        go(rcopy(ref, ref, z_s.at[d, s - 1, cam], z_r.at[d, s - 1, cam], pc.ZP if d == 0 else pc.ZM))

    def z_open(pair):
        for cam in (2 * pair, 2 * pair + 1):
            for d in range(2):
                z_send(d, 1, cam)

    def z_step(pair, s):
        for cam in (2 * pair, 2 * pair + 1):
            for d in range(2):
                if s <= steps(d, cam):
                    ref = z_ref(d, s, cam)
                    rcopy(ref, ref, z_s.at[d, s - 1, cam], z_r.at[d, s - 1, cam], pc.ZP).wait_recv()
                    if s < steps(d, cam):
                        z_send(d, s + 1, cam)

    def go(c):
        c.start()
        sent.append(c)


    def project(pair):
        def one(m, carry):
            rows = X[2 * pair : 2 * pair + 2].reshape(256, HALF)
            acc = jnp.dot(rows, W[m].reshape(HALF, 256), preferred_element_type=F32)
            left, right = acc[:, :128], acc[:, 128:]
            part_s[pair, m] = jnp.where(v == 0, right, left).astype(BF16)
            kept[pair, m] = jnp.where(v == 0, left, right)
            return carry

        lax.fori_loop(1, 3, one, 0)
        go(p_cp(2 * pair, 1))
        go(p_cp(2 * pair + 1, 1))
        lax.fori_loop(0, 1, one, 0)
        go(p_cp(2 * pair, 0))
        go(p_cp(2 * pair + 1, 0))

    def p_cp(cam, i):
        at = (cam // 2, pl.ds(0, 1) if i == 0 else pl.ds(1, 2), pl.ds(128 * (cam % 2), 128))
        return rcopy(part_s.at[at], part_r.at[at], p_s.at[cam, i], p_r.at[cam, i], pc.V)

    def whole(cam, m):
        at = (cam // 2, m, pl.ds(128 * (cam % 2), 128))
        return (kept[at] + part_r[at].astype(F32)).astype(BF16)

    def merge(cam):
        p_cp(cam, 1).wait_recv()
        for m in (1, 2):
            KV[m - 1, cam, t] = whole(cam, m)
        kvrings[cam].start()

    def merge_query(cam):
        p_cp(cam, 0).wait_recv()
        Q[cam] = whole(cam, 0)

    def kv_at(cam):
        return lambda tt, half: KV.at[half, cam, tt]

    kvrings = [RingGather(pc, kv_at(c), k_s.at[c], k_r.at[c]) for c in range(4)]

    def nt(a, b):
        return lax.dot_general(a, b, (((1,), (1,)), ((), ())), preferred_element_type=F32)

    def tn(a, b):
        return lax.dot_general(a, b, (((0,), (0,)), ((), ())), preferred_element_type=F32)

    def keys(m, c):
        return KV[m, c // 2, pl.ds(4 * lax.rem(c, 2), 4)].reshape(512, 128)

    def chunk(c):
        return pl.ds(pl.multiple_of(c * 512, 512), 512)

    def forward(low, high, kp):
        qs = slice(256 * low, 256 * high)
        width = 256 * (high - low)

        def step(c, carry):
            top, total = carry
            s = nt(keys(0, c), Q[2 * low : 2 * high].reshape(width, 128)) * (SCALE * LOG2E)
            block = 8 * lax.rem(c, 2)
            parts = [
                s[64 * e : 64 * e + 64] + bias[c // 2, pl.ds(block + e, 1), qs] for e in range(8)
            ]
            s = jnp.concatenate(parts, axis=0)
            new_top = jnp.maximum(top, jnp.max(s, axis=0, keepdims=True))
            fade = jnp.exp2(top - new_top)
            e = jnp.exp2(s - new_top)
            s_buf[chunk(c), qs] = e
            tops[pl.ds(c, 1), qs] = new_top
            acc[:, qs] = acc[:, qs] * fade + tn(keys(1, c), e.astype(BF16))
            return new_top, total * fade + jnp.sum(e, axis=0, keepdims=True)

        if kp == 0:
            start = (jnp.full((1, width), CLOSED, F32), jnp.zeros((1, width), F32))
            acc[:, qs] = jnp.zeros((128, width), F32)
        else:
            start = (stat[0:1, qs], stat[1:2, qs])
        top, total = lax.fori_loop(4 * kp, 4 * kp + 4, step, start)
        stat[0:1, qs] = top
        stat[1:2, qs] = total

    def settle():
        inv = 1.0 / stat[1:2, :]
        out = jnp.transpose(acc[...] * inv).astype(BF16)
        att[...] = out.reshape(4, 128, 128)
        prod = out.astype(F32) * DO[...].reshape(ROWS, 128).astype(F32)
        acc[...] = jnp.zeros((128, ROWS), F32)
        return inv, jnp.sum(jnp.transpose(prod), axis=0, keepdims=True)

    def back(cam):
        def step(c, carry):
            w = s_buf[chunk(c), :] * (jnp.exp2(tops[pl.ds(c, 1), :] - stat[0:1, :]) * inv)
            g = DO[...].reshape(ROWS, 128)
            dv = jnp.dot(w.astype(BF16), g, preferred_element_type=F32)
            ds = (w * (nt(keys(1, c), g) - delta)).astype(BF16)
            ds_buf[chunk(c), :] = ds
            dk = jnp.dot(ds, Q[...].reshape(ROWS, 128), preferred_element_type=F32) * SCALE
            at = pl.ds(4 * lax.rem(c, 2), 4)
            dkv[0, cam, at] = dk.astype(BF16).reshape(4, 128, 128)
            dkv[1, cam, at] = dv.astype(BF16).reshape(4, 128, 128)
            return carry

        lax.fori_loop(2 * cam, 2 * cam + 2, step, 0)
        for k in range(4):
            drings[cam].sib_send(k)

    def query_back(cam):
        def step(c, carry):
            acc[...] += tn(keys(0, c), ds_buf[chunk(c), :])
            return carry

        lax.fori_loop(2 * cam, 2 * cam + 2, step, 0)

    swapped(0, 1 - v, y)
    swapped(2, 1 - v, y2)
    assemble(1 - v)
    z_open(1 - v)
    swapped(1, v, y2)
    assemble(v)
    z_open(v)
    z_step(0, 1)
    z_step(1, 1)
    z_step(0, 2)
    wring.first()
    z_step(1, 2)
    z_step(0, 3)
    wring.second()
    z_step(1, 3)
    z_step(0, 4)
    wring.finish()
    project(0)
    z_step(1, 4)
    project(1)
    merge(0)
    merge(1)
    kvrings[0].first()
    kvrings[1].first()
    merge(2)
    merge(3)
    kvrings[0].second()
    kvrings[1].second()
    merge_query(0)
    merge_query(1)
    do_copy.wait_recv()
    kvrings[0].finish()
    kvrings[1].finish()
    kvrings[2].first()
    kvrings[3].first()
    forward(0, 1, 0)
    kvrings[2].second()
    kvrings[3].second()
    merge_query(2)
    merge_query(3)
    forward(1, 2, 0)
    kvrings[2].finish()
    kvrings[3].finish()
    forward(0, 2, 1)
    inv, delta = settle()
    def shifted(k):
        return lax.rem(x + (2, 1, 3, 0)[k], 4)

    def make_dring(p):
        return RingScatter(
            pc,
            lambda k, half: dkv[half, p, 2 * shifted(k) + core].astype(F32),
            lambda k: dkv.at[:, p, 2 * shifted(k) + 1 - core],
            sib1.at[p], b1s.at[p], b1r.at[p], d_s.at[p], d_r.at[p],
        )

    drings = [make_dring(p) for p in range(4)]
    own_cols = lanes(v * 128, 128)

    def g_copy(p, m, head):
        rows = pl.ds(0, ROWS) if m == 0 else pl.ds(128 * p, 128)
        ref = G.at[rows, lanes(m * 256 + head * 128, 128)]
        return ref, rcopy(ref, ref, e_s.at[p, m], e_r.at[p, m], pc.V)

    def give(p, m, value):
        ref, c = g_copy(p, m, v)
        ref[...] = value
        go(c)

    def take(p, m):
        g_copy(p, m, 1 - v)[1].wait_recv()

    def hand_on(p):
        for half in range(2):
            give(p, 1 + half, drings[p].last(half).astype(BF16))

    back(0)
    back(1)
    drings[0].far()
    drings[0].near()
    back(2)
    back(3)
    drings[0].near2()
    drings[1].far()
    drings[1].near()
    for cam in range(4):
        query_back(cam)
    give(0, 0, jnp.transpose(acc[...] * SCALE).astype(BF16))
    drings[1].near2()
    hand_on(0)
    drings[2].far()
    drings[2].near()
    drings[3].far()
    drings[3].near()
    hand_on(1)
    drings[2].near2()
    drings[3].near2()
    att_out[:, :, own_cols] = att[pl.ds(2 * v, 2)]

    def token_term(cam, n):
        rows = G[128 * cam : 128 * (cam + n), :]

        def some(i, carry):
            total = jnp.zeros((128 * n, 640), F32)
            for m in range(3):
                weight = W[m, pl.ds(2 * i, 2)].reshape(640, 256)
                total = total + nt(rows[:, 256 * m : 256 * m + 256], weight)
            TG[cam : cam + n, :, :, lanes(i * 640, 640)] = total.reshape(n, 8, 16, 640)
            return carry

        lax.fori_loop(0, 4, some, 0)

    def t_z_cp(d, s, cam):
        return rcopy(
            zbs.at[d, s - 1, cam], zbr.at[d, s - 1, cam], t_s.at[d, s - 1, cam], t_r.at[d, s - 1, cam],
            pc.ZP if d == 0 else pc.ZM,
        )

    def t_step(cam, s):
        for d in range(2):
            n = steps(d, cam)
            if s <= n:
                far = n - s + 1
                value = TG[cam, lax.rem(z + (far if d == 0 else 8 - far), 8)]
                if s > 1:
                    t_z_cp(d, s - 1, cam).wait_recv()
                    value = value + zbr[d, s - 2, cam].astype(F32)
                zbs[d, s - 1, cam] = value.astype(BF16)
                go(t_z_cp(d, s, cam))

    def t_last(cam):
        value = TG[cam, z]
        for d in range(2):
            n = steps(d, cam)
            t_z_cp(d, n, cam).wait_recv()
            value = value + zbr[d, n - 1, cam].astype(F32)
        fin[cam] = value

    def make_gring(m):
        return RingScatter(
            pc,
            lambda k, half: wt[m, k, pl.ds(half * 160, 160)],
            lambda k: sib2s.at[m, k],
            sib2r.at[m], b2s.at[m], b2r.at[m], f_s.at[m], f_r.at[m],
        )

    grings = [make_gring(m) for m in range(3)]

    def weight_term(m):
        for k in range(4):
            cols = X[:, :, :, lanes(shifted(k) * 640, 640)].reshape(ROWS, 640)
            term = tn(cols, G[:, 256 * m : 256 * m + 256])
            low, high = term[:320], term[320:]
            wt[m, k] = jnp.where(core == 0, low, high)
            other = jnp.where(core == 0, high, low).astype(BF16)
            sib2s[m, k, 0] = other[:160]
            sib2s[m, k, 1] = other[160:]
            grings[m].sib_send(k)

    def token_start(cam, n):
        for c in range(cam, cam + n):
            take(c, 1)
            take(c, 2)
        token_term(cam, n)
        for c in range(cam, cam + n):
            t_step(c, 1)

    def weight_out(m, out):
        for half in range(2):
            out[160 * half : 160 * half + 160] = grings[m].last(half).astype(BF16)

    take(0, 0)
    token_start(0, 1)
    hand_on(2)
    token_start(1, 1)
    hand_on(3)
    go(rcopy(att.at[pl.ds(2 - 2 * v, 2)], att_out.at[:, :, own_cols], a_s, a_r, pc.V))
    t_step(0, 2)
    t_step(1, 2)
    token_start(2, 2)
    weight_term(0)
    t_step(0, 3)
    t_step(1, 3)
    grings[0].far()
    weight_term(1)
    t_step(2, 2)
    t_step(3, 2)
    grings[0].near()
    weight_term(2)
    t_step(0, 4)
    t_step(1, 4)
    grings[1].far()
    grings[1].near()
    grings[0].near2()
    t_step(2, 3)
    t_step(3, 3)
    grings[2].far()
    grings[2].near()
    grings[1].near2()
    weight_out(0, gq)
    t_step(2, 4)
    t_step(3, 4)
    grings[2].near2()
    weight_out(1, gk)
    for cam in range(4):
        t_last(cam)

    def piece(vv, yy):
        rows = pl.ds(pl.multiple_of(8 * yy, 8), 8)
        return jnp.concatenate((fin[2 * vv, rows], fin[2 * vv + 1, rows]), axis=0)

    def y_cp(k):
        return rcopy(ys.at[k], yr.at[k], y_s.at[k], y_r.at[k], (pc.V, pc.Y, pc.D)[k])

    for k, (vv, yy) in enumerate(((1 - v, y), (v, 1 - y), (1 - v, 1 - y))):
        ys[k] = piece(vv, yy).astype(BF16)
        go(y_cp(k))
    weight_out(2, gv)
    for k in range(3):
        y_cp(k).wait_recv()
    tgrad[:, lanes(v * HALF, HALF)] = (piece(v, y) + yr[1].astype(F32)).astype(BF16)
    tgrad[:, lanes((1 - v) * HALF, HALF)] = (yr[0].astype(F32) + yr[2].astype(F32)).astype(BF16)
    rcopy(att.at[pl.ds(2 - 2 * v, 2)], att_out.at[:, :, lanes((1 - v) * 128, 128)], a_s, a_r, pc.V).wait_recv()
    for ring in (wring, *kvrings, *drings, *grings):
        ring.end()
    for c in (*swaps, do_copy, *sent):
        c.wait_send()


def hand_over_kernel(*refs):
    ins, outs, held, sems = refs[:5], refs[5:10], refs[10:15], refs[15]
    loads = [pltpu.make_async_copy(ins[i], held[i], sems.at[0, i]) for i in range(5)]
    stores = [pltpu.make_async_copy(held[i], outs[i], sems.at[1, i]) for i in range(5)]
    for c in loads:
        c.start()
    for load, store in zip(loads, stores):
        load.wait()
        store.start()
    for c in stores:
        c.wait()


def on_device(tokens, query_weight, key_weight, value_weight, out_grad, pairs, block_masks):
    vm = pl.BlockSpec(memory_space=pltpu.VMEM)
    sm = pl.BlockSpec(memory_space=pltpu.SMEM)
    hbm = pl.BlockSpec(memory_space=pl.ANY)
    dma = pltpu.SemaphoreType.DMA

    def shape(*dims):
        return jax.ShapeDtypeStruct(dims, BF16)

    def half(*dims):
        return pltpu.VMEM(dims, BF16)

    def full(*dims):
        return pltpu.VMEM(dims, F32)

    outs = pl.pallas_call(
        fused_kernel,
        out_shape=(
            shape(2, 128, 256), shape(16, 2 * HALF), shape(320, 256), shape(320, 256), shape(320, 256),
        ),
        in_specs=[hbm] * 5 + [sm] * 2,
        out_specs=[vm] * 5,
        scratch_shapes=[
            half(4, 8, 16, HALF), half(3, 8, 320, 256), half(4, 128, 128), half(4, 128, 128),
            half(2, 4, 8, 128, 128), half(2, 2, 16, HALF), full(2, 3, 256, 128),
            half(2, 3, 256, 128), half(2, 3, 256, 128),
            full(8, ROWS), full(4, 16, ROWS), full(4096, ROWS), half(4096, ROWS),
            full(16, ROWS), full(8, ROWS),
            full(128, ROWS), half(4, 128, 128), half(2, 4, 8, 128, 128),
            half(ROWS, 768), full(4, 8, 16, HALF), half(2, 4, 4, 16, HALF), half(2, 4, 4, 16, HALF),
            full(4, 16, HALF), half(3, 16, HALF), half(3, 16, HALF),
            half(4, 4, 2, 128, 128), half(4, 6, 128, 128), half(4, 6, 128, 128),
            full(3, 4, 320, 256), half(3, 4, 2, 160, 256), half(3, 4, 2, 160, 256),
            half(3, 6, 160, 256), half(3, 6, 160, 256),
            dma((5,)), dma((3,)), dma((3,)), dma, dma, dma((2, 4, 4)), dma((2, 4, 4)),
            dma((14,)), dma((14,)), dma((4, 14)), dma((4, 14)), dma((4, 2)), dma((4, 2)),
            dma, dma, dma((4, 3)), dma((4, 3)), dma((2, 4, 4)), dma((2, 4, 4)), dma((3,)), dma((3,)),
            dma((4, 10)), dma((4, 10)), dma((3, 10)), dma((3, 10)),
        ],
        compiler_params=pltpu.CompilerParams(
            collective_id=0, has_side_effects=True, vmem_limit_bytes=VMEM_LIMIT
        ),
        name="fused",
    )(
        tokens.reshape(16, 2 * HALF), query_weight, key_weight, value_weight, out_grad, pairs.T,
        block_masks,
    )

    att_out, tgrad, gq, gk, gv = pl.pallas_call(
        hand_over_kernel,
        out_shape=tuple(jax.ShapeDtypeStruct(a.shape, a.dtype) for a in outs),
        in_specs=[hbm] * 5,
        out_specs=[hbm] * 5,
        scratch_shapes=[*(pltpu.VMEM(a.shape, BF16) for a in outs), dma((2, 5))],
        compiler_params=pltpu.CompilerParams(vmem_limit_bytes=VMEM_LIMIT),
        name="hand_over",
    )(*outs)
    return (att_out, tgrad.reshape(2, 8, 2 * HALF), gq, gk, gv)


def solution(mesh):
    return jax.shard_map(
        on_device,
        mesh=mesh,
        in_specs=(
            P("view", ("tm", "head"), None),
            P(("view", "tm"), "head"),
            P(("view", "tm"), "head"),
            P(("view", "tm"), "head"),
            P("view", "tm", "head"),
            P(),
            P(),
        ),
        out_specs=(
            P("view", "tm", "head"),
            P("view", ("tm", "head"), None),
            P(("view", "tm"), "head"),
            P(("view", "tm"), "head"),
            P(("view", "tm"), "head"),
        ),
        check_vma=False,
    )
```

```python
import math

import jax
import jax.numpy as jnp
from jax import lax
from jax.experimental import pallas as pl
from jax.experimental.pallas import tpu as pltpu
from jax.sharding import PartitionSpec as P

MESH = pl.DeviceIdType.MESH
F32 = jnp.float32
BF16 = jnp.bfloat16
VMEM_LIMIT = 58 * 1024 * 1024

HALF = 2560
ROWS = 512
SCALE = 1.0 / math.sqrt(128)
CLOSED = -1e30
LOG2E = math.log2(math.e)


class Place:
    def __init__(self):
        self.v = lax.axis_index("view")
        self.t = lax.axis_index("tm")
        self.h = lax.axis_index("head")
        v, t, h = self.v, self.t, self.h
        self.x, self.core = t // 2, lax.rem(t, 2)
        self.z, self.y = h // 2, lax.rem(h, 2)
        self.sib_t = t + 1 - 2 * self.core
        other_h = h + 1 - 2 * self.y
        self.V = {"view": 1 - v}
        self.Y = {"head": other_h}
        self.D = {"view": 1 - v, "head": other_h}
        self.ZP = {"head": lax.rem(h + 2, 16)}
        self.ZM = {"head": lax.rem(h + 14, 16)}
        self.XP = {"tm": lax.rem(t + 2, 8)}
        self.XM = {"tm": lax.rem(t + 6, 8)}
        self.S = {"tm": self.sib_t}

    def greet(self):
        bar = pltpu.get_barrier_semaphore()
        peers = (self.V, self.Y, self.D, self.ZP, self.ZM, self.XP, self.XM, self.S)
        for peer in peers:
            pl.semaphore_signal(bar, inc=1, device_id=peer, device_id_type=MESH)
        pl.semaphore_wait(bar, len(peers))


def rcopy(src, dst, ss, rs, dev):
    return pltpu.make_async_remote_copy(
        src_ref=src, dst_ref=dst, send_sem=ss, recv_sem=rs, device_id=dev, device_id_type=MESH
    )


def lanes(start, size):
    return pl.ds(pl.multiple_of(start, 128), size)


class RingGather:
    def __init__(self, pc, at, ss, rs):
        self.pc, self.at, self.ss, self.rs = pc, at, ss, rs
        self.sent = []

    def cp(self, i, t, half, dev):
        ref = self.at(t, half)
        return rcopy(ref, ref, self.ss.at[i], self.rs.at[i], dev)

    def send(self, i, off, half, dev):
        c = self.cp(i, lax.rem(self.pc.t + off, 8), half, dev)
        c.start()
        self.sent.append(c)

    def recv(self, i, off, half):
        self.cp(i, lax.rem(self.pc.t + off, 8), half, self.pc.S).wait_recv()

    def recv_sib(self, i, off, half):
        self.cp(i, lax.rem(self.pc.sib_t + off, 8), half, self.pc.S).wait_recv()

    def start(self):
        pc = self.pc
        self.send(0, 0, 0, pc.XP)
        self.send(3, 0, 1, pc.XM)
        self.send(1, 0, 1, pc.XP)
        self.send(2, 0, 0, pc.XM)
        self.send(4, 0, 0, pc.S)
        self.send(5, 0, 1, pc.S)

    def first(self):
        pc = self.pc
        self.recv(0, 6, 0)
        self.send(6, 6, 0, pc.XP)
        self.recv(3, 2, 1)
        self.send(7, 2, 1, pc.XM)
        self.send(8, 6, 0, pc.S)
        self.send(11, 2, 1, pc.S)
        self.recv(1, 6, 1)
        self.send(9, 6, 1, pc.S)
        self.recv(2, 2, 0)
        self.send(10, 2, 0, pc.S)

    def second(self):
        pc = self.pc
        self.recv(6, 4, 0)
        self.send(12, 4, 0, pc.S)
        self.recv(7, 4, 1)
        self.send(13, 4, 1, pc.S)

    def finish(self):
        for i, off, half in (
            (4, 0, 0), (5, 0, 1), (8, 6, 0), (9, 6, 1), (10, 2, 0), (11, 2, 1), (12, 4, 0), (13, 4, 1),
        ):
            self.recv_sib(i, off, half)

    def end(self):
        for c in self.sent:
            c.wait_send()


class RingScatter:
    def __init__(self, pc, own, sib_src, sib_r, bufs, bufr, ss, rs):
        self.pc, self.own, self.sib_src, self.sib_r = pc, own, sib_src, sib_r
        self.bufs, self.bufr, self.ss, self.rs = bufs, bufr, ss, rs
        self.sent = []

    def sib_cp(self, k):
        return rcopy(self.sib_src(k), self.sib_r.at[k], self.ss.at[6 + k], self.rs.at[6 + k], self.pc.S)

    def sib_send(self, k):
        c = self.sib_cp(k)
        c.start()
        self.sent.append(c)

    def sib_wait(self, k):
        self.sib_cp(k).wait_recv()

    def cp(self, i, dev):
        return rcopy(self.bufs.at[i], self.bufr.at[i], self.ss.at[i], self.rs.at[i], dev)

    def term(self, k, half):
        return self.own(k, half) + self.sib_r[k, half].astype(F32)

    def push(self, i, value, dev):
        self.bufs[i] = value.astype(BF16)
        c = self.cp(i, dev)
        c.start()
        self.sent.append(c)

    def wait(self, i):
        self.cp(i, self.pc.S).wait_recv()
        return self.bufr[i].astype(F32)

    def far(self):
        self.sib_wait(0)
        self.push(0, self.term(0, 0), self.pc.XP)
        self.push(1, self.term(0, 1), self.pc.XM)

    def near(self):
        self.sib_wait(1)
        self.push(3, self.term(1, 1), self.pc.XP)
        self.sib_wait(2)
        self.push(4, self.term(2, 0), self.pc.XM)

    def near2(self):
        self.push(2, self.term(1, 0) + self.wait(0), self.pc.XP)
        self.push(5, self.term(2, 1) + self.wait(1), self.pc.XM)

    def last(self, half):
        if half == 0:
            self.sib_wait(3)
        return self.term(3, half) + self.wait(2 + half) + self.wait(4 + half)

    def end(self):
        for c in self.sent:
            c.wait_send()


def fused_kernel(
    tok, wq, wk, wv, dout, pairs, masks,
    att_out, tgrad, gq, gk, gv,
    X, W, Q, DO, KV, stage, kept, part_s, part_r,
    link, bias, s_buf, ds_buf, tops, stat, acc, att, dkv,
    G, TG, zbs, zbr, fin, ys, yr, sib1, b1s, b1r, wt, sib2s, sib2r, b2s, b2r,
    l_s, sw_s, sw_r, do_s, do_r, z_s, z_r, w_s, w_r, k_s, k_r, p_s, p_r,
    a_s, a_r, e_s, e_r, t_s, t_r, y_s, y_r, d_s, d_r, f_s, f_r,
):
    pc = Place()
    v, t, z, y, x, core = pc.v, pc.t, pc.z, pc.y, pc.x, pc.core
    loads = [
        pltpu.make_async_copy(tok.at[:, lanes(v * HALF, HALF)], stage.at[v, y], l_s.at[0]),
        pltpu.make_async_copy(wq, W.at[0, t], l_s.at[1]),
        pltpu.make_async_copy(wk, W.at[1, t], l_s.at[2]),
        pltpu.make_async_copy(wv, W.at[2, t], l_s.at[3]),
        pltpu.make_async_copy(
            dout.at[:, :, lanes(v * 128, 128)], DO.at[pl.ds(2 * v, 2)], l_s.at[4]
        ),
    ]
    for c in loads:
        c.start()
    pc.greet()
    swaps = []
    sent = []
    y2 = 1 - y
    for k, dev, vv in ((0, pc.V, 1 - v), (2, pc.D, 1 - v), (1, pc.Y, v)):
        c = rcopy(tok.at[:, lanes(vv * HALF, HALF)], stage.at[v, y], sw_s.at[k], sw_r.at[k], dev)
        c.start()
        swaps.append(c)

    def w_at(tt, half):
        return W.at[:, tt, pl.ds(half * 160, 160)]

    for c in loads:
        c.wait()
    wring = RingGather(pc, w_at, w_s, w_r)
    wring.start()
    do_copy = rcopy(
        dout.at[:, :, lanes((1 - v) * 128, 128)], DO.at[pl.ds(2 * v, 2)], do_s, do_r, pc.V
    )
    do_copy.start()

    def make_bias():
        for j in range(4):
            for i in range(4):
                hit = jnp.int32(0)
                for r in range(5):
                    a, b = pairs[0, r], pairs[1, r]
                    one = jnp.logical_or(
                        jnp.logical_and(a == i, b == j), jnp.logical_and(a == j, b == i)
                    )
                    hit = hit + one.astype(jnp.int32)
                level = jnp.where(hit > 0, 0.0, CLOSED).astype(F32)
                link[pl.ds(j, 1), pl.ds(128 * i, 128)] = jnp.full((1, 128), level, F32)
        for j in range(4):
            for s in range(16):
                level = jnp.where(masks[j, s] > 0, 0.0, CLOSED).astype(F32)
                bias[j, pl.ds(s, 1), :] = link[pl.ds(j, 1), :] + level

    make_bias()

    def swapped(k, a, b):
        rcopy(stage.at[a, b], stage.at[a, b], sw_s.at[k], sw_r.at[k], pc.V).wait_recv()

    def assemble(vv):
        low = stage[vv, 0].astype(F32)
        high = stage[vv, 1].astype(F32)
        for c in range(2):
            both = jnp.concatenate((low[8 * c : 8 * c + 8], high[8 * c : 8 * c + 8]), axis=0)
            X[2 * vv + c, z] = both.astype(BF16)

    def steps(d, cam):
        return 4 if (d == 0) == (cam < 2) else 3

    def z_ref(d, s, cam):
        return X.at[cam, lax.rem(z + ((8 - s) if d == 0 else s), 8)]

    def z_send(d, s, cam):
        ref = z_ref(d, s - 1, cam)
        go(rcopy(ref, ref, z_s.at[d, s - 1, cam], z_r.at[d, s - 1, cam], pc.ZP if d == 0 else pc.ZM))

    def z_open(pair):
        for cam in (2 * pair, 2 * pair + 1):
            for d in range(2):
                z_send(d, 1, cam)

    def z_step(pair, s):
        for cam in (2 * pair, 2 * pair + 1):
            for d in range(2):
                if s <= steps(d, cam):
                    ref = z_ref(d, s, cam)
                    rcopy(ref, ref, z_s.at[d, s - 1, cam], z_r.at[d, s - 1, cam], pc.ZP).wait_recv()
                    if s < steps(d, cam):
                        z_send(d, s + 1, cam)

    def go(c):
        c.start()
        sent.append(c)


    def project(pair):
        def one(m, carry):
            rows = X[2 * pair : 2 * pair + 2].reshape(256, HALF)
            acc = jnp.dot(rows, W[m].reshape(HALF, 256), preferred_element_type=F32)
            left, right = acc[:, :128], acc[:, 128:]
            part_s[pair, m] = jnp.where(v == 0, right, left).astype(BF16)
            kept[pair, m] = jnp.where(v == 0, left, right)
            return carry

        lax.fori_loop(1, 3, one, 0)
        go(p_cp(2 * pair, 1))
        go(p_cp(2 * pair + 1, 1))
        lax.fori_loop(0, 1, one, 0)
        go(p_cp(2 * pair, 0))
        go(p_cp(2 * pair + 1, 0))

    def p_cp(cam, i):
        at = (cam // 2, pl.ds(0, 1) if i == 0 else pl.ds(1, 2), pl.ds(128 * (cam % 2), 128))
        return rcopy(part_s.at[at], part_r.at[at], p_s.at[cam, i], p_r.at[cam, i], pc.V)

    def whole(cam, m):
        at = (cam // 2, m, pl.ds(128 * (cam % 2), 128))
        return (kept[at] + part_r[at].astype(F32)).astype(BF16)

    def merge(cam):
        p_cp(cam, 1).wait_recv()
        for m in (1, 2):
            KV[m - 1, cam, t] = whole(cam, m)
        kvrings[cam].start()

    def merge_query(cam):
        p_cp(cam, 0).wait_recv()
        Q[cam] = whole(cam, 0)

    def kv_at(cam):
        return lambda tt, half: KV.at[half, cam, tt]

    kvrings = [RingGather(pc, kv_at(c), k_s.at[c], k_r.at[c]) for c in range(4)]

    def nt(a, b):
        return lax.dot_general(a, b, (((1,), (1,)), ((), ())), preferred_element_type=F32)

    def tn(a, b):
        return lax.dot_general(a, b, (((0,), (0,)), ((), ())), preferred_element_type=F32)

    def keys(m, c):
        return KV[m, c].reshape(1024, 128)

    def chunk(c):
        return pl.ds(pl.multiple_of(c * 1024, 1024), 1024)

    def forward(low, high, kp):
        qs = slice(256 * low, 256 * high)
        width = 256 * (high - low)

        def step(c, carry):
            top, total = carry
            s = nt(keys(0, c), Q[2 * low : 2 * high].reshape(width, 128)) * (SCALE * LOG2E)
            parts = [
                s[64 * e : 64 * e + 64] + bias[c, pl.ds(e, 1), qs] for e in range(16)
            ]
            s = jnp.concatenate(parts, axis=0)
            new_top = jnp.maximum(top, jnp.max(s, axis=0, keepdims=True))
            fade = jnp.exp2(top - new_top)
            e = jnp.exp2(s - new_top)
            s_buf[chunk(c), qs] = e
            tops[pl.ds(c, 1), qs] = new_top
            acc[:, qs] = acc[:, qs] * fade + tn(keys(1, c), e.astype(BF16))
            return new_top, total * fade + jnp.sum(e, axis=0, keepdims=True)

        if kp == 0:
            start = (jnp.full((1, width), CLOSED, F32), jnp.zeros((1, width), F32))
            acc[:, qs] = jnp.zeros((128, width), F32)
        else:
            start = (stat[0:1, qs], stat[1:2, qs])
        top, total = lax.fori_loop(2 * kp, 2 * kp + 2, step, start)
        stat[0:1, qs] = top
        stat[1:2, qs] = total

    def settle():
        inv = 1.0 / stat[1:2, :]
        out = jnp.transpose(acc[...] * inv).astype(BF16)
        att[...] = out.reshape(4, 128, 128)
        prod = out.astype(F32) * DO[...].reshape(ROWS, 128).astype(F32)
        return inv, jnp.sum(jnp.transpose(prod), axis=0, keepdims=True)

    def back(cam):
        def step(c, carry):
            w = s_buf[chunk(c), :] * (jnp.exp2(tops[pl.ds(c, 1), :] - stat[0:1, :]) * inv)
            g = DO[...].reshape(ROWS, 128)
            dv = jnp.dot(w.astype(BF16), g, preferred_element_type=F32)
            ds = (w * (nt(keys(1, c), g) - delta)).astype(BF16)
            ds_buf[chunk(c), :] = ds
            dk = jnp.dot(ds, Q[...].reshape(ROWS, 128), preferred_element_type=F32) * SCALE
            dkv[0, cam] = dk.astype(BF16).reshape(8, 128, 128)
            dkv[1, cam] = dv.astype(BF16).reshape(8, 128, 128)
            return carry

        lax.fori_loop(cam, cam + 1, step, 0)
        for k in range(4):
            drings[cam].sib_send(k)

    def query_back():
        total = tn(keys(0, 0), ds_buf[chunk(0), :])
        for c in range(1, 4):
            total = total + tn(keys(0, c), ds_buf[chunk(c), :])
        return jnp.transpose(total * SCALE).astype(BF16)

    swapped(0, 1 - v, y)
    swapped(2, 1 - v, y2)
    assemble(1 - v)
    z_open(1 - v)
    swapped(1, v, y2)
    assemble(v)
    z_open(v)
    z_step(0, 1)
    z_step(1, 1)
    z_step(0, 2)
    wring.first()
    z_step(1, 2)
    z_step(0, 3)
    wring.second()
    z_step(1, 3)
    z_step(0, 4)
    wring.finish()
    project(0)
    z_step(1, 4)
    project(1)
    merge(0)
    merge(1)
    kvrings[0].first()
    kvrings[1].first()
    merge(2)
    merge(3)
    kvrings[0].second()
    kvrings[1].second()
    merge_query(0)
    merge_query(1)
    do_copy.wait_recv()
    kvrings[0].finish()
    kvrings[1].finish()
    kvrings[2].first()
    kvrings[3].first()
    forward(0, 1, 0)
    kvrings[2].second()
    kvrings[3].second()
    merge_query(2)
    merge_query(3)
    forward(1, 2, 0)
    kvrings[2].finish()
    kvrings[3].finish()
    forward(0, 2, 1)
    inv, delta = settle()
    def shifted(k):
        return lax.rem(x + (2, 1, 3, 0)[k], 4)

    def make_dring(p):
        return RingScatter(
            pc,
            lambda k, half: dkv[half, p, 2 * shifted(k) + core].astype(F32),
            lambda k: dkv.at[:, p, 2 * shifted(k) + 1 - core],
            sib1.at[p], b1s.at[p], b1r.at[p], d_s.at[p], d_r.at[p],
        )

    drings = [make_dring(p) for p in range(4)]
    own_cols = lanes(v * 128, 128)

    def g_copy(p, m, head):
        rows = pl.ds(0, ROWS) if m == 0 else pl.ds(128 * p, 128)
        ref = G.at[rows, lanes(m * 256 + head * 128, 128)]
        return ref, rcopy(ref, ref, e_s.at[p, m], e_r.at[p, m], pc.V)

    def give(p, m, value):
        ref, c = g_copy(p, m, v)
        ref[...] = value
        go(c)

    def take(p, m):
        g_copy(p, m, 1 - v)[1].wait_recv()

    def hand_on(p):
        for half in range(2):
            give(p, 1 + half, drings[p].last(half).astype(BF16))

    back(0)
    back(1)
    drings[0].far()
    drings[0].near()
    back(2)
    back(3)
    drings[0].near2()
    drings[1].far()
    drings[1].near()
    give(0, 0, query_back())
    drings[1].near2()
    hand_on(0)
    drings[2].far()
    drings[2].near()
    drings[3].far()
    drings[3].near()
    hand_on(1)
    drings[2].near2()
    drings[3].near2()
    att_out[:, :, own_cols] = att[pl.ds(2 * v, 2)]

    def token_term(cam, n):
        rows = G[128 * cam : 128 * (cam + n), :]

        def some(i, carry):
            total = jnp.zeros((128 * n, 640), F32)
            for m in range(3):
                weight = W[m, pl.ds(2 * i, 2)].reshape(640, 256)
                total = total + nt(rows[:, 256 * m : 256 * m + 256], weight)
            TG[cam : cam + n, :, :, lanes(i * 640, 640)] = total.reshape(n, 8, 16, 640)
            return carry

        lax.fori_loop(0, 4, some, 0)

    def t_z_cp(d, s, cam):
        return rcopy(
            zbs.at[d, s - 1, cam], zbr.at[d, s - 1, cam], t_s.at[d, s - 1, cam], t_r.at[d, s - 1, cam],
            pc.ZP if d == 0 else pc.ZM,
        )

    def t_step(cam, s):
        for d in range(2):
            n = steps(d, cam)
            if s <= n:
                far = n - s + 1
                value = TG[cam, lax.rem(z + (far if d == 0 else 8 - far), 8)]
                if s > 1:
                    t_z_cp(d, s - 1, cam).wait_recv()
                    value = value + zbr[d, s - 2, cam].astype(F32)
                zbs[d, s - 1, cam] = value.astype(BF16)
                go(t_z_cp(d, s, cam))

    def t_last(cam):
        value = TG[cam, z]
        for d in range(2):
            n = steps(d, cam)
            t_z_cp(d, n, cam).wait_recv()
            value = value + zbr[d, n - 1, cam].astype(F32)
        fin[cam] = value

    def make_gring(m):
        return RingScatter(
            pc,
            lambda k, half: wt[m, k, pl.ds(half * 160, 160)],
            lambda k: sib2s.at[m, k],
            sib2r.at[m], b2s.at[m], b2r.at[m], f_s.at[m], f_r.at[m],
        )

    grings = [make_gring(m) for m in range(3)]

    def weight_term(m):
        for k in range(4):
            cols = X[:, :, :, lanes(shifted(k) * 640, 640)].reshape(ROWS, 640)
            term = tn(cols, G[:, 256 * m : 256 * m + 256])
            low, high = term[:320], term[320:]
            wt[m, k] = jnp.where(core == 0, low, high)
            other = jnp.where(core == 0, high, low).astype(BF16)
            sib2s[m, k, 0] = other[:160]
            sib2s[m, k, 1] = other[160:]
            grings[m].sib_send(k)

    def token_start(cam, n):
        for c in range(cam, cam + n):
            take(c, 1)
            take(c, 2)
        token_term(cam, n)
        for c in range(cam, cam + n):
            t_step(c, 1)

    def weight_out(m, out):
        for half in range(2):
            out[160 * half : 160 * half + 160] = grings[m].last(half).astype(BF16)

    take(0, 0)
    token_start(0, 1)
    hand_on(2)
    token_start(1, 1)
    hand_on(3)
    go(rcopy(att.at[pl.ds(2 - 2 * v, 2)], att_out.at[:, :, own_cols], a_s, a_r, pc.V))
    t_step(0, 2)
    t_step(1, 2)
    token_start(2, 2)
    weight_term(0)
    t_step(0, 3)
    t_step(1, 3)
    grings[0].far()
    weight_term(1)
    t_step(2, 2)
    t_step(3, 2)
    grings[0].near()
    weight_term(2)
    t_step(0, 4)
    t_step(1, 4)
    grings[1].far()
    grings[1].near()
    grings[0].near2()
    t_step(2, 3)
    t_step(3, 3)
    grings[2].far()
    grings[2].near()
    grings[1].near2()
    weight_out(0, gq)
    t_step(2, 4)
    t_step(3, 4)
    grings[2].near2()
    weight_out(1, gk)
    for cam in range(4):
        t_last(cam)

    def piece(vv, yy):
        rows = pl.ds(pl.multiple_of(8 * yy, 8), 8)
        return jnp.concatenate((fin[2 * vv, rows], fin[2 * vv + 1, rows]), axis=0)

    def y_cp(k):
        return rcopy(ys.at[k], yr.at[k], y_s.at[k], y_r.at[k], (pc.V, pc.Y, pc.D)[k])

    for k, (vv, yy) in enumerate(((1 - v, y), (v, 1 - y), (1 - v, 1 - y))):
        ys[k] = piece(vv, yy).astype(BF16)
        go(y_cp(k))
    weight_out(2, gv)
    for k in range(3):
        y_cp(k).wait_recv()
    tgrad[:, lanes(v * HALF, HALF)] = (piece(v, y) + yr[1].astype(F32)).astype(BF16)
    tgrad[:, lanes((1 - v) * HALF, HALF)] = (yr[0].astype(F32) + yr[2].astype(F32)).astype(BF16)
    rcopy(att.at[pl.ds(2 - 2 * v, 2)], att_out.at[:, :, lanes((1 - v) * 128, 128)], a_s, a_r, pc.V).wait_recv()
    for ring in (wring, *kvrings, *drings, *grings):
        ring.end()
    for c in (*swaps, do_copy, *sent):
        c.wait_send()


def hand_over_kernel(*refs):
    ins, outs, held, sems = refs[:5], refs[5:10], refs[10:15], refs[15]
    loads = [pltpu.make_async_copy(ins[i], held[i], sems.at[0, i]) for i in range(5)]
    stores = [pltpu.make_async_copy(held[i], outs[i], sems.at[1, i]) for i in range(5)]
    for c in loads:
        c.start()
    for load, store in zip(loads, stores):
        load.wait()
        store.start()
    for c in stores:
        c.wait()


def on_device(tokens, query_weight, key_weight, value_weight, out_grad, pairs, block_masks):
    vm = pl.BlockSpec(memory_space=pltpu.VMEM)
    sm = pl.BlockSpec(memory_space=pltpu.SMEM)
    hbm = pl.BlockSpec(memory_space=pl.ANY)
    dma = pltpu.SemaphoreType.DMA

    def shape(*dims):
        return jax.ShapeDtypeStruct(dims, BF16)

    def half(*dims):
        return pltpu.VMEM(dims, BF16)

    def full(*dims):
        return pltpu.VMEM(dims, F32)

    outs = pl.pallas_call(
        fused_kernel,
        out_shape=(
            shape(2, 128, 256), shape(16, 2 * HALF), shape(320, 256), shape(320, 256), shape(320, 256),
        ),
        in_specs=[hbm] * 5 + [sm] * 2,
        out_specs=[vm] * 5,
        scratch_shapes=[
            half(4, 8, 16, HALF), half(3, 8, 320, 256), half(4, 128, 128), half(4, 128, 128),
            half(2, 4, 8, 128, 128), half(2, 2, 16, HALF), full(2, 3, 256, 128),
            half(2, 3, 256, 128), half(2, 3, 256, 128),
            full(8, ROWS), full(4, 16, ROWS), full(4096, ROWS), half(4096, ROWS),
            full(16, ROWS), full(8, ROWS),
            full(128, ROWS), half(4, 128, 128), half(2, 4, 8, 128, 128),
            half(ROWS, 768), full(4, 8, 16, HALF), half(2, 4, 4, 16, HALF), half(2, 4, 4, 16, HALF),
            full(4, 16, HALF), half(3, 16, HALF), half(3, 16, HALF),
            half(4, 4, 2, 128, 128), half(4, 6, 128, 128), half(4, 6, 128, 128),
            full(3, 4, 320, 256), half(3, 4, 2, 160, 256), half(3, 4, 2, 160, 256),
            half(3, 6, 160, 256), half(3, 6, 160, 256),
            dma((5,)), dma((3,)), dma((3,)), dma, dma, dma((2, 4, 4)), dma((2, 4, 4)),
            dma((14,)), dma((14,)), dma((4, 14)), dma((4, 14)), dma((4, 2)), dma((4, 2)),
            dma, dma, dma((4, 3)), dma((4, 3)), dma((2, 4, 4)), dma((2, 4, 4)), dma((3,)), dma((3,)),
            dma((4, 10)), dma((4, 10)), dma((3, 10)), dma((3, 10)),
        ],
        compiler_params=pltpu.CompilerParams(
            collective_id=0, has_side_effects=True, vmem_limit_bytes=VMEM_LIMIT
        ),
        name="fused",
    )(
        tokens.reshape(16, 2 * HALF), query_weight, key_weight, value_weight, out_grad, pairs.T,
        block_masks,
    )

    att_out, tgrad, gq, gk, gv = pl.pallas_call(
        hand_over_kernel,
        out_shape=tuple(jax.ShapeDtypeStruct(a.shape, a.dtype) for a in outs),
        in_specs=[hbm] * 5,
        out_specs=[hbm] * 5,
        scratch_shapes=[*(pltpu.VMEM(a.shape, BF16) for a in outs), dma((2, 5))],
        compiler_params=pltpu.CompilerParams(vmem_limit_bytes=VMEM_LIMIT),
        name="hand_over",
    )(*outs)
    return (att_out, tgrad.reshape(2, 8, 2 * HALF), gq, gk, gv)


def solution(mesh):
    return jax.shard_map(
        on_device,
        mesh=mesh,
        in_specs=(
            P("view", ("tm", "head"), None),
            P(("view", "tm"), "head"),
            P(("view", "tm"), "head"),
            P(("view", "tm"), "head"),
            P("view", "tm", "head"),
            P(),
            P(),
        ),
        out_specs=(
            P("view", "tm", "head"),
            P("view", ("tm", "head"), None),
            P(("view", "tm"), "head"),
            P(("view", "tm"), "head"),
            P(("view", "tm"), "head"),
        ),
        check_vma=False,
    )
```

```python
import math

import jax
import jax.numpy as jnp
from jax import lax
from jax.experimental import pallas as pl
from jax.experimental.pallas import tpu as pltpu
from jax.sharding import PartitionSpec as P

MESH = pl.DeviceIdType.MESH
F32 = jnp.float32
BF16 = jnp.bfloat16
VMEM_LIMIT = 58 * 1024 * 1024

HALF = 2560
ROWS = 512
SCALE = 1.0 / math.sqrt(128)
CLOSED = -1e30
LOG2E = math.log2(math.e)


class Place:
    def __init__(self):
        self.v = lax.axis_index("view")
        self.t = lax.axis_index("tm")
        self.h = lax.axis_index("head")
        v, t, h = self.v, self.t, self.h
        self.x, self.core = t // 2, lax.rem(t, 2)
        self.z, self.y = h // 2, lax.rem(h, 2)
        self.sib_t = t + 1 - 2 * self.core
        other_h = h + 1 - 2 * self.y
        self.V = {"view": 1 - v}
        self.Y = {"head": other_h}
        self.D = {"view": 1 - v, "head": other_h}
        self.ZP = {"head": lax.rem(h + 2, 16)}
        self.ZM = {"head": lax.rem(h + 14, 16)}
        self.XP = {"tm": lax.rem(t + 2, 8)}
        self.XM = {"tm": lax.rem(t + 6, 8)}
        self.S = {"tm": self.sib_t}

    def greet(self):
        bar = pltpu.get_barrier_semaphore()
        peers = (self.V, self.Y, self.D, self.ZP, self.ZM, self.XP, self.XM, self.S)
        for peer in peers:
            pl.semaphore_signal(bar, inc=1, device_id=peer, device_id_type=MESH)
        pl.semaphore_wait(bar, len(peers))


def rcopy(src, dst, ss, rs, dev):
    return pltpu.make_async_remote_copy(
        src_ref=src, dst_ref=dst, send_sem=ss, recv_sem=rs, device_id=dev, device_id_type=MESH
    )


def lanes(start, size):
    return pl.ds(pl.multiple_of(start, 128), size)


class RingGather:
    def __init__(self, pc, at, ss, rs):
        self.pc, self.at, self.ss, self.rs = pc, at, ss, rs
        self.sent = []

    def cp(self, i, t, half, dev):
        ref = self.at(t, half)
        return rcopy(ref, ref, self.ss.at[i], self.rs.at[i], dev)

    def send(self, i, off, half, dev):
        c = self.cp(i, lax.rem(self.pc.t + off, 8), half, dev)
        c.start()
        self.sent.append(c)

    def recv(self, i, off, half):
        self.cp(i, lax.rem(self.pc.t + off, 8), half, self.pc.S).wait_recv()

    def recv_sib(self, i, off, half):
        self.cp(i, lax.rem(self.pc.sib_t + off, 8), half, self.pc.S).wait_recv()

    def start(self):
        pc = self.pc
        self.send(0, 0, 0, pc.XP)
        self.send(3, 0, 1, pc.XM)
        self.send(1, 0, 1, pc.XP)
        self.send(2, 0, 0, pc.XM)
        self.send(4, 0, 0, pc.S)
        self.send(5, 0, 1, pc.S)

    def first(self):
        pc = self.pc
        self.recv(0, 6, 0)
        self.send(6, 6, 0, pc.XP)
        self.recv(3, 2, 1)
        self.send(7, 2, 1, pc.XM)
        self.send(8, 6, 0, pc.S)
        self.send(11, 2, 1, pc.S)
        self.recv(1, 6, 1)
        self.send(9, 6, 1, pc.S)
        self.recv(2, 2, 0)
        self.send(10, 2, 0, pc.S)

    def second(self):
        pc = self.pc
        self.recv(6, 4, 0)
        self.send(12, 4, 0, pc.S)
        self.recv(7, 4, 1)
        self.send(13, 4, 1, pc.S)

    def finish(self):
        for i, off, half in (
            (4, 0, 0), (5, 0, 1), (8, 6, 0), (9, 6, 1), (10, 2, 0), (11, 2, 1), (12, 4, 0), (13, 4, 1),
        ):
            self.recv_sib(i, off, half)

    def end(self):
        for c in self.sent:
            c.wait_send()


class RingScatter:
    def __init__(self, pc, own, sib_src, sib_r, bufs, bufr, ss, rs):
        self.pc, self.own, self.sib_src, self.sib_r = pc, own, sib_src, sib_r
        self.bufs, self.bufr, self.ss, self.rs = bufs, bufr, ss, rs
        self.sent = []

    def sib_cp(self, k):
        return rcopy(self.sib_src(k), self.sib_r.at[k], self.ss.at[6 + k], self.rs.at[6 + k], self.pc.S)

    def sib_send(self, k):
        c = self.sib_cp(k)
        c.start()
        self.sent.append(c)

    def sib_wait(self, k):
        self.sib_cp(k).wait_recv()

    def cp(self, i, dev):
        return rcopy(self.bufs.at[i], self.bufr.at[i], self.ss.at[i], self.rs.at[i], dev)

    def term(self, k, half):
        return self.own(k, half) + self.sib_r[k, half].astype(F32)

    def push(self, i, value, dev):
        self.bufs[i] = value.astype(BF16)
        c = self.cp(i, dev)
        c.start()
        self.sent.append(c)

    def wait(self, i):
        self.cp(i, self.pc.S).wait_recv()
        return self.bufr[i].astype(F32)

    def far(self):
        self.sib_wait(0)
        self.push(0, self.term(0, 0), self.pc.XP)
        self.push(1, self.term(0, 1), self.pc.XM)

    def near(self):
        self.sib_wait(1)
        self.push(3, self.term(1, 1), self.pc.XP)
        self.sib_wait(2)
        self.push(4, self.term(2, 0), self.pc.XM)

    def near2(self):
        self.push(2, self.term(1, 0) + self.wait(0), self.pc.XP)
        self.push(5, self.term(2, 1) + self.wait(1), self.pc.XM)

    def last(self, half):
        if half == 0:
            self.sib_wait(3)
        return self.term(3, half) + self.wait(2 + half) + self.wait(4 + half)

    def end(self):
        for c in self.sent:
            c.wait_send()


def fused_kernel(
    tok, wq, wk, wv, dout, pairs, masks,
    att_out, tgrad, gq, gk, gv,
    X, W, Q, DO, KV, stage, kept, part_s, part_r,
    link, bias, s_buf, ds_buf, tops, stat, acc, att, dkv,
    G, TG, zbs, zbr, fin, ys, yr, sib1, b1s, b1r, wt, sib2s, sib2r, b2s, b2r,
    l_s, sw_s, sw_r, do_s, do_r, z_s, z_r, w_s, w_r, k_s, k_r, p_s, p_r,
    a_s, a_r, e_s, e_r, t_s, t_r, y_s, y_r, d_s, d_r, f_s, f_r,
):
    pc = Place()
    v, t, z, y, x, core = pc.v, pc.t, pc.z, pc.y, pc.x, pc.core
    loads = [
        pltpu.make_async_copy(tok.at[:, lanes(v * HALF, HALF)], stage.at[v, y], l_s.at[0]),
        pltpu.make_async_copy(wq, W.at[0, t], l_s.at[1]),
        pltpu.make_async_copy(wk, W.at[1, t], l_s.at[2]),
        pltpu.make_async_copy(wv, W.at[2, t], l_s.at[3]),
        pltpu.make_async_copy(
            dout.at[:, :, lanes(v * 128, 128)], DO.at[pl.ds(2 * v, 2)], l_s.at[4]
        ),
    ]
    for c in loads:
        c.start()
    pc.greet()
    swaps = []
    sent = []
    y2 = 1 - y
    for k, dev, vv in ((0, pc.V, 1 - v), (2, pc.D, 1 - v), (1, pc.Y, v)):
        c = rcopy(tok.at[:, lanes(vv * HALF, HALF)], stage.at[v, y], sw_s.at[k], sw_r.at[k], dev)
        c.start()
        swaps.append(c)

    def w_at(tt, half):
        return W.at[:, tt, pl.ds(half * 160, 160)]

    for c in loads:
        c.wait()
    wring = RingGather(pc, w_at, w_s, w_r)
    wring.start()
    do_copy = rcopy(
        dout.at[:, :, lanes((1 - v) * 128, 128)], DO.at[pl.ds(2 * v, 2)], do_s, do_r, pc.V
    )
    do_copy.start()

    def make_bias():
        for j in range(4):
            for i in range(4):
                hit = jnp.int32(0)
                for r in range(5):
                    a, b = pairs[0, r], pairs[1, r]
                    one = jnp.logical_or(
                        jnp.logical_and(a == i, b == j), jnp.logical_and(a == j, b == i)
                    )
                    hit = hit + one.astype(jnp.int32)
                level = jnp.where(hit > 0, 0.0, CLOSED).astype(F32)
                link[pl.ds(j, 1), pl.ds(128 * i, 128)] = jnp.full((1, 128), level, F32)
        for j in range(4):
            for s in range(16):
                level = jnp.where(masks[j, s] > 0, 0.0, CLOSED).astype(F32)
                bias[j, pl.ds(s, 1), :] = link[pl.ds(j, 1), :] + level

    make_bias()

    def swapped(k, a, b):
        rcopy(stage.at[a, b], stage.at[a, b], sw_s.at[k], sw_r.at[k], pc.V).wait_recv()

    def assemble(vv):
        low = stage[vv, 0].astype(F32)
        high = stage[vv, 1].astype(F32)
        for c in range(2):
            both = jnp.concatenate((low[8 * c : 8 * c + 8], high[8 * c : 8 * c + 8]), axis=0)
            X[2 * vv + c, z] = both.astype(BF16)

    def steps(d, cam):
        return 4 if (d == 0) == (cam < 2) else 3

    def z_ref(d, s, cam):
        return X.at[cam, lax.rem(z + ((8 - s) if d == 0 else s), 8)]

    def z_send(d, s, cam):
        ref = z_ref(d, s - 1, cam)
        go(rcopy(ref, ref, z_s.at[d, s - 1, cam], z_r.at[d, s - 1, cam], pc.ZP if d == 0 else pc.ZM))

    def z_open(pair):
        for cam in (2 * pair, 2 * pair + 1):
            for d in range(2):
                z_send(d, 1, cam)

    def z_step(pair, s):
        for cam in (2 * pair, 2 * pair + 1):
            for d in range(2):
                if s <= steps(d, cam):
                    ref = z_ref(d, s, cam)
                    rcopy(ref, ref, z_s.at[d, s - 1, cam], z_r.at[d, s - 1, cam], pc.ZP).wait_recv()
                    if s < steps(d, cam):
                        z_send(d, s + 1, cam)

    def go(c):
        c.start()
        sent.append(c)


    def project(pair):
        def one(m, carry):
            rows = X[2 * pair : 2 * pair + 2].reshape(256, HALF)
            acc = jnp.dot(rows, W[m].reshape(HALF, 256), preferred_element_type=F32)
            left, right = acc[:, :128], acc[:, 128:]
            part_s[pair, m] = jnp.where(v == 0, right, left).astype(BF16)
            kept[pair, m] = jnp.where(v == 0, left, right)
            return carry

        lax.fori_loop(1, 3, one, 0, unroll=True)
        go(p_cp(2 * pair, 1))
        go(p_cp(2 * pair + 1, 1))
        lax.fori_loop(0, 1, one, 0)
        go(p_cp(2 * pair, 0))
        go(p_cp(2 * pair + 1, 0))

    def p_cp(cam, i):
        at = (cam // 2, pl.ds(0, 1) if i == 0 else pl.ds(1, 2), pl.ds(128 * (cam % 2), 128))
        return rcopy(part_s.at[at], part_r.at[at], p_s.at[cam, i], p_r.at[cam, i], pc.V)

    def whole(cam, m):
        at = (cam // 2, m, pl.ds(128 * (cam % 2), 128))
        return (kept[at] + part_r[at].astype(F32)).astype(BF16)

    def merge(cam):
        p_cp(cam, 1).wait_recv()
        for m in (1, 2):
            KV[m - 1, cam, t] = whole(cam, m)
        kvrings[cam].start()

    def merge_query(cam):
        p_cp(cam, 0).wait_recv()
        Q[cam] = whole(cam, 0)

    def kv_at(cam):
        return lambda tt, half: KV.at[half, cam, tt]

    kvrings = [RingGather(pc, kv_at(c), k_s.at[c], k_r.at[c]) for c in range(4)]

    def nt(a, b):
        return lax.dot_general(a, b, (((1,), (1,)), ((), ())), preferred_element_type=F32)

    def tn(a, b):
        return lax.dot_general(a, b, (((0,), (0,)), ((), ())), preferred_element_type=F32)

    def keys(m, c):
        return KV[m, c].reshape(1024, 128)

    def chunk(c):
        return pl.ds(pl.multiple_of(c * 1024, 1024), 1024)

    def forward(low, high, kp):
        qs = slice(256 * low, 256 * high)
        width = 256 * (high - low)

        def step(c, carry):
            top, total = carry
            s = nt(keys(0, c), Q[2 * low : 2 * high].reshape(width, 128)) * (SCALE * LOG2E)
            parts = [
                s[64 * e : 64 * e + 64] + bias[c, pl.ds(e, 1), qs] for e in range(16)
            ]
            s = jnp.concatenate(parts, axis=0)
            new_top = jnp.maximum(top, jnp.max(s, axis=0, keepdims=True))
            fade = jnp.exp2(top - new_top)
            e = jnp.exp2(s - new_top)
            s_buf[chunk(c), qs] = e
            tops[pl.ds(c, 1), qs] = new_top
            acc[:, qs] = acc[:, qs] * fade + tn(keys(1, c), e.astype(BF16))
            return new_top, total * fade + jnp.sum(e, axis=0, keepdims=True)

        if kp == 0:
            start = (jnp.full((1, width), CLOSED, F32), jnp.zeros((1, width), F32))
            acc[:, qs] = jnp.zeros((128, width), F32)
        else:
            start = (stat[0:1, qs], stat[1:2, qs])
        top, total = lax.fori_loop(2 * kp, 2 * kp + 2, step, start, unroll=True)
        stat[0:1, qs] = top
        stat[1:2, qs] = total

    def settle():
        inv = 1.0 / stat[1:2, :]
        out = jnp.transpose(acc[...] * inv).astype(BF16)
        att[...] = out.reshape(4, 128, 128)
        prod = out.astype(F32) * DO[...].reshape(ROWS, 128).astype(F32)
        return inv, jnp.sum(jnp.transpose(prod), axis=0, keepdims=True)

    def back(cam):
        def step(c, carry):
            w = s_buf[chunk(c), :] * (jnp.exp2(tops[pl.ds(c, 1), :] - stat[0:1, :]) * inv)
            g = DO[...].reshape(ROWS, 128)
            dv = jnp.dot(w.astype(BF16), g, preferred_element_type=F32)
            ds = (w * (nt(keys(1, c), g) - delta)).astype(BF16)
            ds_buf[chunk(c), :] = ds
            dk = jnp.dot(ds, Q[...].reshape(ROWS, 128), preferred_element_type=F32) * SCALE
            dkv[0, cam] = dk.astype(BF16).reshape(8, 128, 128)
            dkv[1, cam] = dv.astype(BF16).reshape(8, 128, 128)
            return carry

        lax.fori_loop(cam, cam + 1, step, 0)
        for k in range(4):
            drings[cam].sib_send(k)

    def query_back():
        total = tn(keys(0, 0), ds_buf[chunk(0), :])
        for c in range(1, 4):
            total = total + tn(keys(0, c), ds_buf[chunk(c), :])
        return jnp.transpose(total * SCALE).astype(BF16)

    swapped(0, 1 - v, y)
    swapped(2, 1 - v, y2)
    assemble(1 - v)
    z_open(1 - v)
    swapped(1, v, y2)
    assemble(v)
    z_open(v)
    z_step(0, 1)
    z_step(1, 1)
    z_step(0, 2)
    wring.first()
    z_step(1, 2)
    z_step(0, 3)
    wring.second()
    z_step(1, 3)
    z_step(0, 4)
    wring.finish()
    project(0)
    z_step(1, 4)
    project(1)
    merge(0)
    merge(1)
    kvrings[0].first()
    kvrings[1].first()
    merge(2)
    merge(3)
    kvrings[0].second()
    kvrings[1].second()
    merge_query(0)
    merge_query(1)
    do_copy.wait_recv()
    kvrings[0].finish()
    kvrings[1].finish()
    kvrings[2].first()
    kvrings[3].first()
    forward(0, 1, 0)
    kvrings[2].second()
    kvrings[3].second()
    merge_query(2)
    merge_query(3)
    forward(1, 2, 0)
    kvrings[2].finish()
    kvrings[3].finish()
    forward(0, 2, 1)
    inv, delta = settle()
    def shifted(k):
        return lax.rem(x + (2, 1, 3, 0)[k], 4)

    def make_dring(p):
        return RingScatter(
            pc,
            lambda k, half: dkv[half, p, 2 * shifted(k) + core].astype(F32),
            lambda k: dkv.at[:, p, 2 * shifted(k) + 1 - core],
            sib1.at[p], b1s.at[p], b1r.at[p], d_s.at[p], d_r.at[p],
        )

    drings = [make_dring(p) for p in range(4)]
    own_cols = lanes(v * 128, 128)

    def g_copy(p, m, head):
        rows = pl.ds(0, ROWS) if m == 0 else pl.ds(128 * p, 128)
        ref = G.at[rows, lanes(m * 256 + head * 128, 128)]
        return ref, rcopy(ref, ref, e_s.at[p, m], e_r.at[p, m], pc.V)

    def give(p, m, value):
        ref, c = g_copy(p, m, v)
        ref[...] = value
        go(c)

    def take(p, m):
        g_copy(p, m, 1 - v)[1].wait_recv()

    def hand_on(p):
        for half in range(2):
            give(p, 1 + half, drings[p].last(half).astype(BF16))

    back(0)
    back(1)
    drings[0].far()
    drings[0].near()
    back(2)
    back(3)
    drings[0].near2()
    drings[1].far()
    drings[1].near()
    give(0, 0, query_back())
    drings[1].near2()
    hand_on(0)
    drings[2].far()
    drings[2].near()
    drings[3].far()
    drings[3].near()
    hand_on(1)
    drings[2].near2()
    drings[3].near2()
    att_out[:, :, own_cols] = att[pl.ds(2 * v, 2)]

    def token_term(cam, n):
        rows = G[128 * cam : 128 * (cam + n), :]

        def some(i, carry):
            total = jnp.zeros((128 * n, 640), F32)
            for m in range(3):
                weight = W[m, pl.ds(2 * i, 2)].reshape(640, 256)
                total = total + nt(rows[:, 256 * m : 256 * m + 256], weight)
            TG[cam : cam + n, :, :, lanes(i * 640, 640)] = total.reshape(n, 8, 16, 640)
            return carry

        lax.fori_loop(0, 4, some, 0, unroll=True)

    def t_z_cp(d, s, cam):
        return rcopy(
            zbs.at[d, s - 1, cam], zbr.at[d, s - 1, cam], t_s.at[d, s - 1, cam], t_r.at[d, s - 1, cam],
            pc.ZP if d == 0 else pc.ZM,
        )

    def t_step(cam, s):
        for d in range(2):
            n = steps(d, cam)
            if s <= n:
                far = n - s + 1
                value = TG[cam, lax.rem(z + (far if d == 0 else 8 - far), 8)]
                if s > 1:
                    t_z_cp(d, s - 1, cam).wait_recv()
                    value = value + zbr[d, s - 2, cam].astype(F32)
                zbs[d, s - 1, cam] = value.astype(BF16)
                go(t_z_cp(d, s, cam))

    def t_last(cam):
        value = TG[cam, z]
        for d in range(2):
            n = steps(d, cam)
            t_z_cp(d, n, cam).wait_recv()
            value = value + zbr[d, n - 1, cam].astype(F32)
        fin[cam] = value

    def make_gring(m):
        return RingScatter(
            pc,
            lambda k, half: wt[m, k, pl.ds(half * 160, 160)],
            lambda k: sib2s.at[m, k],
            sib2r.at[m], b2s.at[m], b2r.at[m], f_s.at[m], f_r.at[m],
        )

    grings = [make_gring(m) for m in range(3)]

    def weight_term(m):
        for k in range(4):
            cols = X[:, :, :, lanes(shifted(k) * 640, 640)].reshape(ROWS, 640)
            term = tn(cols, G[:, 256 * m : 256 * m + 256])
            low, high = term[:320], term[320:]
            wt[m, k] = jnp.where(core == 0, low, high)
            other = jnp.where(core == 0, high, low).astype(BF16)
            sib2s[m, k, 0] = other[:160]
            sib2s[m, k, 1] = other[160:]
            grings[m].sib_send(k)

    def token_start(cam, n):
        for c in range(cam, cam + n):
            take(c, 1)
            take(c, 2)
        token_term(cam, n)
        for c in range(cam, cam + n):
            t_step(c, 1)

    def weight_out(m, out):
        for half in range(2):
            out[160 * half : 160 * half + 160] = grings[m].last(half).astype(BF16)

    take(0, 0)
    token_start(0, 1)
    hand_on(2)
    token_start(1, 1)
    hand_on(3)
    go(rcopy(att.at[pl.ds(2 - 2 * v, 2)], att_out.at[:, :, own_cols], a_s, a_r, pc.V))
    t_step(0, 2)
    t_step(1, 2)
    token_start(2, 2)
    weight_term(0)
    t_step(0, 3)
    t_step(1, 3)
    grings[0].far()
    weight_term(1)
    t_step(2, 2)
    t_step(3, 2)
    grings[0].near()
    weight_term(2)
    t_step(0, 4)
    t_step(1, 4)
    grings[1].far()
    grings[1].near()
    grings[0].near2()
    t_step(2, 3)
    t_step(3, 3)
    grings[2].far()
    grings[2].near()
    grings[1].near2()
    weight_out(0, gq)
    t_step(2, 4)
    t_step(3, 4)
    grings[2].near2()
    weight_out(1, gk)
    for cam in range(4):
        t_last(cam)

    def piece(vv, yy):
        rows = pl.ds(pl.multiple_of(8 * yy, 8), 8)
        return jnp.concatenate((fin[2 * vv, rows], fin[2 * vv + 1, rows]), axis=0)

    def y_cp(k):
        return rcopy(ys.at[k], yr.at[k], y_s.at[k], y_r.at[k], (pc.V, pc.Y, pc.D)[k])

    for k, (vv, yy) in enumerate(((1 - v, y), (v, 1 - y), (1 - v, 1 - y))):
        ys[k] = piece(vv, yy).astype(BF16)
        go(y_cp(k))
    weight_out(2, gv)
    for k in range(3):
        y_cp(k).wait_recv()
    tgrad[:, lanes(v * HALF, HALF)] = (piece(v, y) + yr[1].astype(F32)).astype(BF16)
    tgrad[:, lanes((1 - v) * HALF, HALF)] = (yr[0].astype(F32) + yr[2].astype(F32)).astype(BF16)
    rcopy(att.at[pl.ds(2 - 2 * v, 2)], att_out.at[:, :, lanes((1 - v) * 128, 128)], a_s, a_r, pc.V).wait_recv()
    for ring in (wring, *kvrings, *drings, *grings):
        ring.end()
    for c in (*swaps, do_copy, *sent):
        c.wait_send()


def hand_over_kernel(*refs):
    ins, outs, held, sems = refs[:5], refs[5:10], refs[10:15], refs[15]
    loads = [pltpu.make_async_copy(ins[i], held[i], sems.at[0, i]) for i in range(5)]
    stores = [pltpu.make_async_copy(held[i], outs[i], sems.at[1, i]) for i in range(5)]
    for c in loads:
        c.start()
    for load, store in zip(loads, stores):
        load.wait()
        store.start()
    for c in stores:
        c.wait()


def on_device(tokens, query_weight, key_weight, value_weight, out_grad, pairs, block_masks):
    vm = pl.BlockSpec(memory_space=pltpu.VMEM)
    sm = pl.BlockSpec(memory_space=pltpu.SMEM)
    hbm = pl.BlockSpec(memory_space=pl.ANY)
    dma = pltpu.SemaphoreType.DMA

    def shape(*dims):
        return jax.ShapeDtypeStruct(dims, BF16)

    def half(*dims):
        return pltpu.VMEM(dims, BF16)

    def full(*dims):
        return pltpu.VMEM(dims, F32)

    outs = pl.pallas_call(
        fused_kernel,
        out_shape=(
            shape(2, 128, 256), shape(16, 2 * HALF), shape(320, 256), shape(320, 256), shape(320, 256),
        ),
        in_specs=[hbm] * 5 + [sm] * 2,
        out_specs=[vm] * 5,
        scratch_shapes=[
            half(4, 8, 16, HALF), half(3, 8, 320, 256), half(4, 128, 128), half(4, 128, 128),
            half(2, 4, 8, 128, 128), half(2, 2, 16, HALF), full(2, 3, 256, 128),
            half(2, 3, 256, 128), half(2, 3, 256, 128),
            full(8, ROWS), full(4, 16, ROWS), full(4096, ROWS), half(4096, ROWS),
            full(16, ROWS), full(8, ROWS),
            full(128, ROWS), half(4, 128, 128), half(2, 4, 8, 128, 128),
            half(ROWS, 768), full(4, 8, 16, HALF), half(2, 4, 4, 16, HALF), half(2, 4, 4, 16, HALF),
            full(4, 16, HALF), half(3, 16, HALF), half(3, 16, HALF),
            half(4, 4, 2, 128, 128), half(4, 6, 128, 128), half(4, 6, 128, 128),
            full(3, 4, 320, 256), half(3, 4, 2, 160, 256), half(3, 4, 2, 160, 256),
            half(3, 6, 160, 256), half(3, 6, 160, 256),
            dma((5,)), dma((3,)), dma((3,)), dma, dma, dma((2, 4, 4)), dma((2, 4, 4)),
            dma((14,)), dma((14,)), dma((4, 14)), dma((4, 14)), dma((4, 2)), dma((4, 2)),
            dma, dma, dma((4, 3)), dma((4, 3)), dma((2, 4, 4)), dma((2, 4, 4)), dma((3,)), dma((3,)),
            dma((4, 10)), dma((4, 10)), dma((3, 10)), dma((3, 10)),
        ],
        compiler_params=pltpu.CompilerParams(
            collective_id=0, has_side_effects=True, vmem_limit_bytes=VMEM_LIMIT
        ),
        name="fused",
    )(
        tokens.reshape(16, 2 * HALF), query_weight, key_weight, value_weight, out_grad, pairs.T,
        block_masks,
    )

    att_out, tgrad, gq, gk, gv = pl.pallas_call(
        hand_over_kernel,
        out_shape=tuple(jax.ShapeDtypeStruct(a.shape, a.dtype) for a in outs),
        in_specs=[hbm] * 5,
        out_specs=[hbm] * 5,
        scratch_shapes=[*(pltpu.VMEM(a.shape, BF16) for a in outs), dma((2, 5))],
        compiler_params=pltpu.CompilerParams(vmem_limit_bytes=VMEM_LIMIT),
        name="hand_over",
    )(*outs)
    return (att_out, tgrad.reshape(2, 8, 2 * HALF), gq, gk, gv)


def solution(mesh):
    return jax.shard_map(
        on_device,
        mesh=mesh,
        in_specs=(
            P("view", ("tm", "head"), None),
            P(("view", "tm"), "head"),
            P(("view", "tm"), "head"),
            P(("view", "tm"), "head"),
            P("view", "tm", "head"),
            P(),
            P(),
        ),
        out_specs=(
            P("view", "tm", "head"),
            P("view", ("tm", "head"), None),
            P(("view", "tm"), "head"),
            P(("view", "tm"), "head"),
            P(("view", "tm"), "head"),
        ),
        check_vma=False,
    )
```
